32 devices in a mesh: section: 4 (over y, x), tensor: 8 (over z, core).
Axes of the slice: x: 2, y: 2, z: 4, core: 2. Of those that a mesh axis runs over, the one named last changes fastest.
Arguments:
- hidden: bfloat16 [512, 16384], P('section', 'tensor')
- norm_gain: float32 [16384], P('tensor'), may hold values from 0.3 to 3
- head_weight: bfloat16 [16384, 8192], P(None, ('section', 'tensor'))
- tile_list: int32 [512, 16], replicated, may hold values from 0 to 63, as said below
- tile_count: int32 [512], replicated, may hold values from 1 to 16, as said below
- chosen_token: int32 [512], replicated, may hold values from 0 to 8191, as said below
- chosen_embed: bfloat16 [512, 16384], P('section', 'tensor'), may hold values from -6 to 6
- stack_state: int32 [512], P('section'), may hold values from 0 to 511
- state_table: bfloat16 [512, 16384], P(None, 'tensor'), may hold values from -6 to 6
Outputs:
- log_prob: float32 [512], replicated
- normalizer: float32 [512], replicated
- next_input: bfloat16 [512, 16384], P('section', 'tensor')
The draws below stay inside these ranges and needn't reach their ends.
Inputs may be any that keep to these rules, and one draw needn't show every extreme that they name: `tile_list`: each row lists 16 different tiles; the first tile_count of them are its allowed tiles, the rest are tiles it does not allow. `tile_count`: some row has 16 allowed tiles and some row one. `chosen_token`: each chosen token lies in one of its row's allowed tiles.
All inputs are finite; a program needn't handle non-finite values.
Results may differ from the reference program's by a relative error of at most 0.0035.
Values may be sent and summed in bfloat16 or wider, within the bound.
A program may use at most 64 MiB of HBM per device.

```python
import math
import jax
import jax.numpy as jnp
from jax import lax

D = 16384
TILE = 128
ROWS = 512
STATES = 512
NTILES = 64
VOCAB = 8192
A_MAX = 16
N_SECTION = 4


def tile_draw(key):
    keys = jax.random.split(jax.random.fold_in(key, 11), 5)
    popular_count = max(NTILES // 16, 1)
    popular = jax.random.permutation(keys[0], NTILES)[:popular_count]
    tile_ids = jnp.arange(NTILES, dtype=jnp.int32)
    is_popular = jnp.any(tile_ids[:, None] == popular[None, :], axis=1).astype(jnp.int32)
    scores = jax.random.randint(keys[1], (ROWS, NTILES), 0, 4096) - 3072 * is_popular[None, :]
    keyed = scores * NTILES + tile_ids[None, :]
    order = jnp.argsort(keyed, axis=1)
    tile_list = order[:, :A_MAX].astype(jnp.int32)
    counts = jax.random.randint(keys[2], (ROWS,), 1, A_MAX + 1).astype(jnp.int32)
    counts = counts.at[0].set(A_MAX).at[1].set(1)
    slot = jax.random.randint(keys[3], (ROWS,), 0, 1 << 20) % counts
    tile_pick = jnp.take_along_axis(tile_list, slot[:, None], axis=1)[:, 0]
    chosen = (tile_pick * TILE + jax.random.randint(keys[4], (ROWS,), 0, TILE)).astype(jnp.int32)
    return (tile_list, counts, chosen)


def draw_tile_list(key, part):
    return tile_draw(key)[0]


def draw_tile_count(key, part):
    return tile_draw(key)[1]


def draw_chosen_token(key, part):
    return tile_draw(key)[2]


def draw_hidden(key, part):
    keys = jax.random.split(jax.random.fold_in(key, 31), 3)
    row_scale = jnp.exp(jax.random.uniform(keys[0], (ROWS,), jnp.float32, 0.0, math.log(10.0)))
    column_scale = jnp.exp(jax.random.uniform(keys[1], (D,), jnp.float32, 0.0, math.log(10.0)))
    values = jax.random.normal(keys[2], (ROWS, D), jnp.float32) * row_scale[:, None] * column_scale[None, :]
    return values.astype(jnp.bfloat16)


def draw_head_weight(key, part):
    keys = jax.random.split(jax.random.fold_in(key, 41), 1)
    spread = 3.0 / math.sqrt(D)
    weight = jax.random.normal(keys[0], (D, VOCAB), jnp.float32) * spread
    return weight.astype(jnp.bfloat16)


def place_ends(values, key, least, top_value):
    place = [jax.random.randint(jax.random.fold_in(key, axis), (), 0, length) for axis, length in enumerate(values.shape)]
    widest = values.shape.index(max(values.shape))
    beside = place[:widest] + [(place[widest] + 1) % values.shape[widest]] + place[widest + 1:]
    return values.at[tuple(place)].set(least).at[tuple(beside)].set(top_value)


def steps_of(key, extent, cuts, low, high):
    def one(dim, parts):
        draws = jax.random.uniform(jax.random.fold_in(jax.random.fold_in(key, 6), dim), (parts,), jnp.float32, low / len(cuts), high / len(cuts))
        return jnp.repeat(jnp.exp(draws), extent[dim] // parts).reshape((-1,) + (1,) * (len(extent) - dim - 1))

    level = one(*cuts[0])
    for cut in cuts[1:]:
        level = level * one(*cut)
    return level


def noise(rng, extent, scale, reach, shards=(), kind=jnp.bfloat16):
    loudness = steps_of(rng, extent, shards, -0.22, 0.18) if shards else 1.0
    drawn = jax.random.normal(rng, extent, jnp.float32) * scale * loudness
    return jnp.minimum(jnp.maximum(drawn, -reach), reach).astype(kind)


def setup_inputs(seed: int = 0) -> dict:
    arg_keys = jax.random.split(jax.random.key(seed), 10)
    return {
        "hidden": draw_hidden(jax.random.fold_in(arg_keys[9], 71), 0),
        "norm_gain": jnp.clip(jnp.exp(math.log(3.0) - 2.3025851 * jax.random.uniform(arg_keys[1], (D,), jnp.float32) ** steps_of(arg_keys[1], (D,), ((0, 8),), -0.2, 0.2)), 0.3, 3.0),
        "head_weight": draw_head_weight(jax.random.fold_in(arg_keys[9], 71), 0),
        "tile_list": draw_tile_list(jax.random.fold_in(arg_keys[9], 71), 0),
        "tile_count": draw_tile_count(jax.random.fold_in(arg_keys[9], 71), 0),
        "chosen_token": draw_chosen_token(jax.random.fold_in(arg_keys[9], 71), 0),
        "chosen_embed": noise(arg_keys[6], (ROWS, D), 1.0, 6.0, ((0, 4), (1, 8))),
        "stack_state": place_ends(jax.random.randint(arg_keys[7], (ROWS,), 0, STATES), jax.random.fold_in(arg_keys[7], 1), 0, STATES - 1).astype(jnp.int32),
        "state_table": noise(arg_keys[8], (STATES, D), 1.0, 6.0, ((1, 8),)),
    }


EPSILON = 1e-05

def reference(hidden, norm_gain, head_weight, tile_list, tile_count, chosen_token, chosen_embed, stack_state, state_table):
    widened = hidden.astype(jnp.float32)
    mean_square = lax.optimization_barrier(jnp.mean(widened * widened, axis=1, keepdims=True))
    normed = (widened * lax.rsqrt(mean_square + EPSILON) * norm_gain[None, :]).astype(jnp.bfloat16)
    logits = jnp.dot(normed, head_weight, preferred_element_type=jnp.float32)
    tile_ids = jnp.arange(NTILES, dtype=jnp.int32)
    live_slot = jnp.arange(A_MAX, dtype=jnp.int32)[None, :] < tile_count[:, None]
    matches = (tile_list[:, :, None] == tile_ids[None, None, :]) & live_slot[:, :, None]
    allowed = jnp.any(matches, axis=1)
    blocks = logits.reshape(ROWS, NTILES, TILE)
    allowed_mask = jnp.broadcast_to(allowed[:, :, None], blocks.shape)
    row_top = lax.optimization_barrier(jnp.max(jnp.where(allowed_mask, blocks, -jnp.inf), axis=(1, 2)))
    shifted = jnp.where(allowed_mask, blocks - row_top[:, None, None], -jnp.inf)
    totals = lax.optimization_barrier(jnp.sum(jnp.exp(shifted), axis=(1, 2)))
    normalizer = row_top + jnp.log(totals)
    picked = jnp.take_along_axis(logits, chosen_token[:, None].astype(jnp.int32), axis=1)[:, 0]
    log_prob = picked - normalizer
    states = jnp.arange(STATES, dtype=jnp.int32)
    one_hot = (stack_state[:, None] == states[None, :]).astype(jnp.bfloat16)
    state_rows = jnp.dot(one_hot, state_table, preferred_element_type=jnp.float32)
    merged = (chosen_embed.astype(jnp.float32) + state_rows).astype(jnp.bfloat16)
    next_input = jnp.roll(merged, ROWS // N_SECTION, axis=0)
    return (log_prob, normalizer, next_input)
```

```python
import functools

import jax
import jax.numpy as jnp
from jax import lax
from jax.experimental import pallas as pl
from jax.experimental.pallas import tpu as pltpu
from jax.sharding import PartitionSpec as P

D = 16384
TILE = 128
TILES_DEV = 2


EPSILON = 1e-05
NEG_FILL = -1e30


def shifted_2(value, axis, steps):
    count = lax.axis_size(axis)
    pairs = [(source, (source + steps) % count) for source in range(count)]
    return lax.ppermute(value, axis, pairs)


def scale_rows(widened, squares_total, width, gain):
    factor = lax.rsqrt(squares_total / width + EPSILON)
    return (widened * factor[:, None] * gain[None, :]).astype(jnp.bfloat16)


def shards(
    hidden,
    norm_gain,
    head_weight,
    tile_list,
    tile_count,
    chosen_token,
    chosen_embed,
    stack_state,
    state_table,
):
    states = jnp.arange(state_table.shape[0], dtype=jnp.int32)
    one_hot = (stack_state[:, None] == states[None, :]).astype(jnp.bfloat16)
    state_rows = jnp.dot(one_hot, state_table, preferred_element_type=jnp.float32)
    merged = (chosen_embed.astype(jnp.float32) + state_rows).astype(jnp.bfloat16)
    next_input = shifted_2(merged, "section", 1)
    widened = hidden.astype(jnp.float32)
    squares_total = lax.psum(jnp.sum(widened * widened, axis=1), "tensor")
    normed = scale_rows(widened, squares_total, D, norm_gain)
    all_rows = lax.all_gather(normed, "section", axis=0, tiled=True)
    logits = jnp.dot(
        lax.all_gather(all_rows, "tensor", axis=1, tiled=True),
        head_weight,
        preferred_element_type=jnp.float32,
    )
    row_count = logits.shape[0]
    vocab_here = logits.shape[1]
    device = lax.axis_index("section") * lax.axis_size("tensor") + lax.axis_index("tensor")
    own_tiles = device * TILES_DEV + jnp.arange(TILES_DEV, dtype=jnp.int32)
    live_slot = jnp.arange(tile_list.shape[1], dtype=jnp.int32)[None, :] < tile_count[:, None]
    matches = (tile_list[:, :, None] == own_tiles[None, None, :]) & live_slot[:, :, None]
    allowed = jnp.any(matches, axis=1)
    blocks = logits.reshape(row_count, TILES_DEV, TILE)
    allowed_mask = jnp.broadcast_to(allowed[:, :, None], blocks.shape)
    local_top = jnp.max(jnp.where(allowed_mask, blocks, NEG_FILL), axis=(1, 2))
    column = chosen_token - device * vocab_here
    columns = jnp.arange(vocab_here, dtype=jnp.int32)
    picked = jnp.sum(jnp.where(columns[None, :] == column[:, None], logits, 0.0), axis=1)
    row_top = lax.pmax(local_top, ("section", "tensor"))
    shifted = jnp.where(allowed_mask, blocks - row_top[:, None, None], NEG_FILL)
    terms = jnp.sum(jnp.exp(shifted), axis=(1, 2))
    totals, chosen_logit = lax.psum((terms, picked), ("section", "tensor"))
    normalizer = row_top + jnp.log(totals)
    log_prob = chosen_logit - normalizer
    return (log_prob, normalizer, next_input)


LOWEST = -3e38
MESH = pl.DeviceIdType.MESH
ANY = pl.BlockSpec(memory_space=pl.ANY)
VMEM = pl.BlockSpec(memory_space=pltpu.VMEM)


def head_kernel(
    hidden_hbm,
    gain_ref,
    weight_hbm,
    tiles_ref,
    count_ref,
    token_ref,
    embed_hbm,
    state_ref,
    table_hbm,
    log_prob_ref,
    normalizer_ref,
    next_hbm,
    rows_all,
    weight,
    total,
    hidden,
    embed,
    table,
    merged,
    parts,
    plane_stats,
    line_stats,
    send_sems,
    line_sems,
    recv_sems,
    next_sem,
    parts_sems,
    plane_sems,
    line_stat_sems,
    local_sems,
):
    section = lax.axis_index("section")
    tensor = lax.axis_index("tensor")
    sections = 4
    tensors = 8
    x, y = section % 2, section // 2
    z, core = tensor // 2, tensor % 2
    beside_x = section + 1 - 2 * x
    beside_y = section + 2 - 4 * y
    across = 3 - section
    twin = tensor + 1 - 2 * core
    height, width = hidden.shape
    half = height // 2
    columns = weight.shape[1]
    device = section * tensors + tensor

    reads = [
        pltpu.make_async_copy(source, target, local_sems.at[n])
        for n, (source, target) in enumerate(
            ((hidden_hbm, hidden), (table_hbm, table), (embed_hbm, embed), (weight_hbm, weight))
        )
    ]
    for read in reads:
        read.start()

    plane = [((section + k // 2) % sections, (tensor // 2) * 2 + (core + k) % 2) for k in range(1, 8)]
    line = [(section, (tensor + k) % tensors) for k in range(1, 8)]
    barrier = pltpu.get_barrier_semaphore()
    greeted = plane + [(section, ((z + k) % 4) * 2 + c) for k in range(1, 4) for c in range(2)]
    for peer in greeted:
        pl.semaphore_signal(barrier, inc=1, device_id=peer, device_id_type=MESH)

    reads[0].wait()
    widened = hidden[...].astype(jnp.float32)
    squares = jnp.sum(widened * widened, axis=1, keepdims=True)
    laid = jnp.transpose(jnp.broadcast_to(squares, (height, 128)))[0:8, :]
    parts[pl.ds(tensor, 1)] = laid[None]
    pl.semaphore_wait(barrier, len(greeted))

    unconditional = []
    conditional = []

    def push(source, target, receive, peer, when=None):
        if when is None:
            copy = pltpu.make_async_remote_copy(
                src_ref=source,
                dst_ref=target,
                send_sem=send_sems.at[len(unconditional)],
                recv_sem=receive,
                device_id=peer,
                device_id_type=MESH,
            )
            unconditional.append(copy)
            copy.start()
        else:
            copy = pltpu.make_async_remote_copy(
                src_ref=source,
                dst_ref=target,
                send_sem=line_sems.at[len(conditional)],
                recv_sem=receive,
                device_id=peer,
                device_id_type=MESH,
            )
            conditional.append((when, copy))
            pl.when(when)(copy.start)

    def arrived(target, receive):
        pltpu.make_async_remote_copy(
            src_ref=target,
            dst_ref=target,
            send_sem=send_sems.at[0],
            recv_sem=receive,
            device_id=(section, twin),
            device_id_type=MESH,
        ).wait_recv()

    for peer in line:
        push(parts.at[tensor], parts.at[tensor], parts_sems.at[tensor], peer)

    states = lax.broadcasted_iota(jnp.int32, (table.shape[0], height), 0)
    one_hot = jnp.transpose((states == state_ref[...]).astype(jnp.float32)).astype(jnp.bfloat16)
    reads[1].wait()
    reads[2].wait()
    state_rows = jnp.dot(one_hot, table[...], preferred_element_type=jnp.float32)
    merged[...] = (embed[...].astype(jnp.float32) + state_rows).astype(jnp.bfloat16)
    push(merged, next_hbm, next_sem, ((section + 1) % sections, tensor))

    for _, peer in line:
        arrived(parts.at[peer], parts_sems.at[peer])
    squares_total = jnp.sum(parts[...], axis=0)[0:1, :]
    factor = lax.rsqrt(squares_total / (width * tensors) + EPSILON)
    factor = jnp.transpose(jnp.broadcast_to(factor, (128, height)))[:, 0:1]
    own = section * tensors + tensor
    rows_all[pl.ds(own, 1)] = (hidden[...].astype(jnp.float32) * factor * gain_ref[...]).astype(jnp.bfloat16)[None]

    top, low = pl.ds(0, half), pl.ds(half, half)
    total[...] = jnp.zeros_like(total)

    def multiply(from_section, from_tensor):
        row = pl.ds(pl.multiple_of(from_section * height, height), height)
        feature = pl.ds(pl.multiple_of(from_tensor * width, width), width)
        total[row, :] += jnp.dot(
            rows_all[from_section * tensors + from_tensor], weight[feature, :], preferred_element_type=jnp.float32
        )

    upper = z // 2
    order = []
    mirrored = z + upper * (3 - 2 * z)
    for place in (mirrored, 1 - mirrored, 2, 3):
        order.append(place + upper * (3 - 2 * place))

    def to_twin(block):
        push(rows_all.at[block], rows_all.at[block], recv_sems.at[block, 0], (section, twin))

    def from_line(step):
        place = order[step]
        block = section * tensors + place * 2 + core
        whole = rows_all.at[block]
        if step:
            arrived(whole, recv_sems.at[block, 0])
        push(whole, whole, recv_sems.at[block, 0], (section, tensor + 2), (place <= z) & (z < 3))
        push(whole, whole, recv_sems.at[block, 0], (section, tensor - 2), (place >= z) & (z > 0))
        for peer, parts_in_order in ((beside_x, (0, 1)), (beside_y, (1, 0))):
            for part in parts_in_order:
                piece = rows_all.at[block, (top, low)[part]]
                push(piece, piece, recv_sems.at[block, part], (peer, tensor))
        to_twin(block)
        if step == 0:
            reads[3].wait()
        multiply(section, place * 2 + core)

    def from_beside(step):
        column = order[step] * 2 + core
        for source, onward, part in ((beside_x, beside_y, 0), (beside_y, beside_x, 1)):
            block = source * tensors + column
            piece = rows_all.at[block, (top, low)[part]]
            arrived(piece, recv_sems.at[block, part])
            push(piece, piece, recv_sems.at[block, part], (onward, tensor))
        for source, part in ((beside_x, 1), (beside_y, 0)):
            block = source * tensors + column
            piece = rows_all.at[block, (top, low)[part]]
            arrived(piece, recv_sems.at[block, part])
            to_twin(block)
        multiply(beside_x, column)
        multiply(beside_y, column)

    def from_across(step):
        column = order[step] * 2 + core
        block = across * tensors + column
        for part in range(2):
            arrived(rows_all.at[block, (top, low)[part]], recv_sems.at[block, part])
        to_twin(block)
        multiply(across, column)

    def from_twin(sources, step):
        column = order[step] * 2 + 1 - core
        for source in sources:
            block = source * tensors + column
            arrived(rows_all.at[block], recv_sems.at[block, 0])
            multiply(source, column)

    aside = (beside_x, beside_y)
    from_line(0)
    from_beside(0)
    from_line(1)
    from_twin((section,), 0)
    from_twin(aside, 0)
    from_across(0)
    from_line(2)
    from_twin((section,), 1)
    from_twin((across,), 0)
    from_beside(1)
    from_line(3)
    from_twin(aside, 1)
    from_twin((section,), 2)
    from_across(1)
    from_beside(2)
    from_twin((across,), 1)
    from_twin((section,), 3)
    from_twin(aside, 2)
    from_across(2)
    from_beside(3)
    from_twin((across,), 2)
    from_twin(aside, 3)
    from_across(3)
    from_twin((across,), 3)

    logits = jnp.transpose(total[...])
    slots = lax.broadcasted_iota(jnp.int32, tiles_ref.shape, 0)
    live = slots < count_ref[...]
    own_tiles = columns // TILE
    hits = []
    for n in range(own_tiles):
        match = live & (tiles_ref[...] == device * own_tiles + n)
        hits.append(jnp.max(match.astype(jnp.int32), axis=0, keepdims=True) > 0)
    blocks = [logits[n * TILE:(n + 1) * TILE, :] for n in range(own_tiles)]
    largest = jnp.full(count_ref.shape, LOWEST, jnp.float32)
    for hit, block in zip(hits, blocks):
        largest = jnp.maximum(largest, jnp.where(hit, jnp.max(block, axis=0, keepdims=True), LOWEST))
    terms = jnp.zeros_like(largest)
    for hit, block in zip(hits, blocks):
        terms += jnp.where(hit, jnp.sum(jnp.exp(block - largest), axis=0, keepdims=True), 0.0)
    place = lax.broadcasted_iota(jnp.int32, logits.shape, 0)
    chosen = jnp.sum(jnp.where(place == token_ref[...] - device * columns, logits, 0.0), axis=0, keepdims=True)

    def packed(largest, terms, chosen):
        line = lax.broadcasted_iota(jnp.int32, (8, largest.shape[1]), 0)
        return jnp.where(line == 0, largest, jnp.where(line == 1, terms, jnp.where(line == 2, chosen, 0.0)))

    def combined(stats):
        values = [stats[n] for n in range(stats.shape[0])]
        largest = functools.reduce(jnp.maximum, [value[0:1, :] for value in values])
        terms = sum(value[1:2, :] * jnp.exp(value[0:1, :] - largest) for value in values)
        chosen = sum(value[2:3, :] for value in values)
        return largest, terms, chosen

    slot = section * 2 + core
    plane_stats[pl.ds(slot, 1)] = packed(largest, terms, chosen)[None]
    for peer in plane:
        push(plane_stats.at[slot], plane_stats.at[slot], plane_sems.at[slot], peer)
    for peer_section, peer_tensor in plane:
        peer_slot = peer_section * 2 + peer_tensor % 2
        arrived(plane_stats.at[peer_slot], plane_sems.at[peer_slot])
    line_stats[pl.ds(z, 1)] = packed(*combined(plane_stats))[None]
    for k in range(1, 4):
        push(line_stats.at[z], line_stats.at[z], line_stat_sems.at[z], (section, ((z + k) % 4) * 2 + core))
    for k in range(1, 4):
        peer_z = (z + k) % 4
        arrived(line_stats.at[peer_z], line_stat_sems.at[peer_z])
    largest, terms, chosen = combined(line_stats)
    normalizer = largest + jnp.log(terms)
    normalizer_ref[...] = normalizer
    log_prob_ref[...] = chosen - normalizer

    arrived(next_hbm, next_sem)
    for copy in unconditional:
        copy.wait_send()
    for when, copy in conditional:
        pl.when(when)(copy.wait_send)


def block_shards(
    hidden,
    norm_gain,
    head_weight,
    tile_list,
    tile_count,
    chosen_token,
    chosen_embed,
    stack_state,
    state_table,
):
    height, width = hidden.shape
    row_count = tile_count.shape[0]
    dma = pltpu.SemaphoreType.DMA
    log_prob, normalizer, next_input = pl.pallas_call(
        head_kernel,
        out_shape=(
            jax.ShapeDtypeStruct((1, row_count), jnp.float32),
            jax.ShapeDtypeStruct((1, row_count), jnp.float32),
            jax.ShapeDtypeStruct(chosen_embed.shape, jnp.bfloat16),
        ),
        in_specs=[ANY, VMEM, ANY, VMEM, VMEM, VMEM, ANY, VMEM, ANY],
        out_specs=(VMEM, VMEM, ANY),
        scratch_shapes=[
            pltpu.VMEM((32, height, width), jnp.bfloat16),
            pltpu.VMEM(head_weight.shape, jnp.bfloat16),
            pltpu.VMEM((row_count, head_weight.shape[1]), jnp.float32),
            pltpu.VMEM(hidden.shape, jnp.bfloat16),
            pltpu.VMEM(chosen_embed.shape, jnp.bfloat16),
            pltpu.VMEM(state_table.shape, jnp.bfloat16),
            pltpu.VMEM(chosen_embed.shape, jnp.bfloat16),
            pltpu.VMEM((8, 8, height), jnp.float32),
            pltpu.VMEM((8, 8, row_count), jnp.float32),
            pltpu.VMEM((4, 8, row_count), jnp.float32),
            dma((80,)),
            dma((8,)),
            dma((32, 2)),
            dma,
            dma((8,)),
            dma((8,)),
            dma((4,)),
            dma((4,)),
        ],
        compiler_params=pltpu.CompilerParams(
            collective_id=0, has_side_effects=True, vmem_limit_bytes=48 * 1024 * 1024
        ),
        name="masked_head",
    )(
        hidden,
        norm_gain[None, :],
        head_weight,
        tile_list.T,
        tile_count[None, :],
        chosen_token[None, :],
        chosen_embed,
        stack_state[None, :],
        state_table,
    )
    return (log_prob[0], normalizer[0], next_input)


def solution(mesh):
    placed = (
        P("section", "tensor"),
        P("tensor"),
        P(None, ("section", "tensor")),
        P(),
        P(),
        P(),
        P("section", "tensor"),
        P("section"),
        P(None, "tensor"),
    )
    small = mesh.shape["section"] == 4 and mesh.shape["tensor"] == 8
    return jax.shard_map(
        block_shards if small else shards,
        mesh=mesh,
        in_specs=placed,
        out_specs=(P(), P(), P("section", "tensor")),
        check_vma=False,
    )
```

```python
import functools

import jax
import jax.numpy as jnp
from jax import lax
from jax.experimental import pallas as pl
from jax.experimental.pallas import tpu as pltpu
from jax.sharding import PartitionSpec as P

D = 16384
TILE = 128
TILES_DEV = 2


EPSILON = 1e-05
NEG_FILL = -1e30


def shifted_2(value, axis, steps):
    count = lax.axis_size(axis)
    pairs = [(source, (source + steps) % count) for source in range(count)]
    return lax.ppermute(value, axis, pairs)


def scale_rows(widened, squares_total, width, gain):
    factor = lax.rsqrt(squares_total / width + EPSILON)
    return (widened * factor[:, None] * gain[None, :]).astype(jnp.bfloat16)


def shards(
    hidden,
    norm_gain,
    head_weight,
    tile_list,
    tile_count,
    chosen_token,
    chosen_embed,
    stack_state,
    state_table,
):
    states = jnp.arange(state_table.shape[0], dtype=jnp.int32)
    one_hot = (stack_state[:, None] == states[None, :]).astype(jnp.bfloat16)
    state_rows = jnp.dot(one_hot, state_table, preferred_element_type=jnp.float32)
    merged = (chosen_embed.astype(jnp.float32) + state_rows).astype(jnp.bfloat16)
    next_input = shifted_2(merged, "section", 1)
    widened = hidden.astype(jnp.float32)
    squares_total = lax.psum(jnp.sum(widened * widened, axis=1), "tensor")
    normed = scale_rows(widened, squares_total, D, norm_gain)
    all_rows = lax.all_gather(normed, "section", axis=0, tiled=True)
    logits = jnp.dot(
        lax.all_gather(all_rows, "tensor", axis=1, tiled=True),
        head_weight,
        preferred_element_type=jnp.float32,
    )
    row_count = logits.shape[0]
    vocab_here = logits.shape[1]
    device = lax.axis_index("section") * lax.axis_size("tensor") + lax.axis_index("tensor")
    own_tiles = device * TILES_DEV + jnp.arange(TILES_DEV, dtype=jnp.int32)
    live_slot = jnp.arange(tile_list.shape[1], dtype=jnp.int32)[None, :] < tile_count[:, None]
    matches = (tile_list[:, :, None] == own_tiles[None, None, :]) & live_slot[:, :, None]
    allowed = jnp.any(matches, axis=1)
    blocks = logits.reshape(row_count, TILES_DEV, TILE)
    allowed_mask = jnp.broadcast_to(allowed[:, :, None], blocks.shape)
    local_top = jnp.max(jnp.where(allowed_mask, blocks, NEG_FILL), axis=(1, 2))
    column = chosen_token - device * vocab_here
    columns = jnp.arange(vocab_here, dtype=jnp.int32)
    picked = jnp.sum(jnp.where(columns[None, :] == column[:, None], logits, 0.0), axis=1)
    row_top = lax.pmax(local_top, ("section", "tensor"))
    shifted = jnp.where(allowed_mask, blocks - row_top[:, None, None], NEG_FILL)
    terms = jnp.sum(jnp.exp(shifted), axis=(1, 2))
    totals, chosen_logit = lax.psum((terms, picked), ("section", "tensor"))
    normalizer = row_top + jnp.log(totals)
    log_prob = chosen_logit - normalizer
    return (log_prob, normalizer, next_input)


LOWEST = -3e38
MESH = pl.DeviceIdType.MESH
HBM = pl.BlockSpec(memory_space=pltpu.HBM)
VMEM = pl.BlockSpec(memory_space=pltpu.VMEM)


def head_kernel(
    hidden_hbm,
    gain_hbm,
    weight_hbm,
    tiles_hbm,
    count_hbm,
    token_hbm,
    embed_hbm,
    state_hbm,
    table_hbm,
    log_prob_ref,
    normalizer_ref,
    next_hbm,
    rows_all,
    weight,
    total,
    hidden,
    embed,
    table,
    merged,
    gain_ref,
    tiles_ref,
    count_ref,
    token_ref,
    state_ref,
    parts,
    plane_stats,
    line_stats,
    send_sems,
    line_sems,
    recv_sems,
    next_sem,
    parts_sems,
    plane_sems,
    line_stat_sems,
    local_sems,
):
    section = lax.axis_index("section")
    tensor = lax.axis_index("tensor")
    sections = 4
    tensors = 8
    x, y = section % 2, section // 2
    z, core = tensor // 2, tensor % 2
    beside_x = section + 1 - 2 * x
    beside_y = section + 2 - 4 * y
    across = 3 - section
    twin = tensor + 1 - 2 * core
    height, width = hidden.shape
    columns = weight.shape[1]
    device = section * tensors + tensor

    reads = [
        pltpu.make_async_copy(source, target, local_sems.at[n])
        for n, (source, target) in enumerate(
            (
                (hidden_hbm, hidden),
                (table_hbm, table),
                (embed_hbm, embed),
                (weight_hbm, weight),
                (state_hbm, state_ref),
                (gain_hbm, gain_ref),
                (tiles_hbm, tiles_ref),
                (count_hbm, count_ref),
                (token_hbm, token_ref),
            )
        )
    ]
    for read in reads:
        read.start()

    plane = [((section + k // 2) % sections, (tensor // 2) * 2 + (core + k) % 2) for k in range(1, 8)]
    line = [(section, (tensor + k) % tensors) for k in range(1, 8)]
    barrier = pltpu.get_barrier_semaphore()
    greeted = plane + [(section, ((z + k) % 4) * 2 + c) for k in range(1, 4) for c in range(2)]
    for peer in greeted:
        pl.semaphore_signal(barrier, inc=1, device_id=peer, device_id_type=MESH)

    reads[0].wait()
    widened = hidden[...].astype(jnp.float32)
    squares = jnp.sum(widened * widened, axis=1, keepdims=True)
    laid = jnp.transpose(jnp.broadcast_to(squares, (height, 128)))[0:8, :]
    parts[pl.ds(tensor, 1)] = laid[None]
    pl.semaphore_wait(barrier, len(greeted))

    unconditional = []
    conditional = []

    def push(source, target, receive, peer, when=None):
        if when is None:
            copy = pltpu.make_async_remote_copy(
                src_ref=source,
                dst_ref=target,
                send_sem=send_sems.at[len(unconditional)],
                recv_sem=receive,
                device_id=peer,
                device_id_type=MESH,
            )
            unconditional.append(copy)
            copy.start()
        else:
            copy = pltpu.make_async_remote_copy(
                src_ref=source,
                dst_ref=target,
                send_sem=line_sems.at[len(conditional)],
                recv_sem=receive,
                device_id=peer,
                device_id_type=MESH,
            )
            conditional.append((when, copy))
            pl.when(when)(copy.start)

    def arrived(target, receive):
        pltpu.make_async_remote_copy(
            src_ref=target,
            dst_ref=target,
            send_sem=send_sems.at[0],
            recv_sem=receive,
            device_id=(section, twin),
            device_id_type=MESH,
        ).wait_recv()

    for peer in line:
        push(parts.at[tensor], parts.at[tensor], parts_sems.at[tensor], peer)

    reads[4].wait()
    states = lax.broadcasted_iota(jnp.int32, (table.shape[0], height), 0)
    one_hot = jnp.transpose((states == state_ref[...]).astype(jnp.float32)).astype(jnp.bfloat16)
    reads[1].wait()
    reads[2].wait()
    state_rows = jnp.dot(one_hot, table[...], preferred_element_type=jnp.float32)
    merged[...] = (embed[...].astype(jnp.float32) + state_rows).astype(jnp.bfloat16)
    push(merged, next_hbm, next_sem, ((section + 1) % sections, tensor))

    for _, peer in line:
        arrived(parts.at[peer], parts_sems.at[peer])
    squares_total = jnp.sum(parts[...], axis=0)[0:1, :]
    reads[5].wait()
    factor = lax.rsqrt(squares_total / (width * tensors) + EPSILON)
    factor = jnp.transpose(jnp.broadcast_to(factor, (128, height)))[:, 0:1]
    own = section * tensors + tensor
    rows_all[pl.ds(own, 1)] = (hidden[...].astype(jnp.float32) * factor * gain_ref[...]).astype(jnp.bfloat16)[None]

    first = height * 3 // 4
    tail = pl.ds(first, height - first)

    def halves(step):
        size = (first if step else height) // 2
        return pl.ds(0, size), pl.ds(size, size)

    total[...] = jnp.zeros_like(total)

    def multiply(from_section, from_tensor):
        row = pl.ds(pl.multiple_of(from_section * height, height), height)
        feature = pl.ds(pl.multiple_of(from_tensor * width, width), width)
        total[row, :] += jnp.dot(
            rows_all[from_section * tensors + from_tensor], weight[feature, :], preferred_element_type=jnp.float32
        )

    upper = z // 2
    order = []
    mirrored = z + upper * (3 - 2 * z)
    for place in (mirrored, 1 - mirrored, 2, 3):
        order.append(place + upper * (3 - 2 * place))

    def to_twin(block):
        push(rows_all.at[block], rows_all.at[block], recv_sems.at[block, 0], (section, twin))

    def along(piece, receive, place):
        push(piece, piece, receive, (section, tensor + 2), (place <= z) & (z < 3))
        push(piece, piece, receive, (section, tensor - 2), (place >= z) & (z > 0))

    def from_line(step):
        place = order[step]
        block = section * tensors + place * 2 + core
        whole = rows_all.at[block]
        if step:
            arrived(whole, recv_sems.at[block, 0])
        along(whole, recv_sems.at[block, 0], place)
        for peer, parts_in_order in ((beside_x, (0, 1)), (beside_y, (1, 0))):
            for part in parts_in_order:
                piece = rows_all.at[block, halves(step)[part]]
                push(piece, piece, recv_sems.at[block, part], (peer, tensor))
        to_twin(block)
        if step == 0:
            reads[3].wait()
        multiply(section, place * 2 + core)

    def tails(sources, step):
        for source in sources:
            block = source * tensors + order[step] * 2 + core
            piece = rows_all.at[block, tail]
            if step:
                arrived(piece, recv_sems.at[block, 2])
            along(piece, recv_sems.at[block, 2], order[step])

    def from_beside(step):
        column = order[step] * 2 + core
        for source, onward, part in ((beside_x, beside_y, 0), (beside_y, beside_x, 1)):
            block = source * tensors + column
            piece = rows_all.at[block, halves(step)[part]]
            arrived(piece, recv_sems.at[block, part])
            push(piece, piece, recv_sems.at[block, part], (onward, tensor))
        for source, part in ((beside_x, 1), (beside_y, 0)):
            block = source * tensors + column
            piece = rows_all.at[block, halves(step)[part]]
            arrived(piece, recv_sems.at[block, part])
            if step == 0:
                tails((source,), 0)
            to_twin(block)
        multiply(beside_x, column)
        multiply(beside_y, column)

    def from_across(step):
        column = order[step] * 2 + core
        block = across * tensors + column
        for part in range(2):
            arrived(rows_all.at[block, halves(step)[part]], recv_sems.at[block, part])
        if step == 0:
            tails((across,), 0)
        to_twin(block)
        multiply(across, column)

    def from_twin(sources, step):
        column = order[step] * 2 + 1 - core
        for source in sources:
            block = source * tensors + column
            arrived(rows_all.at[block], recv_sems.at[block, 0])
            multiply(source, column)

    aside = (beside_x, beside_y)
    others = (beside_x, beside_y, across)
    from_line(0)
    from_beside(0)
    from_line(1)
    from_across(0)
    from_twin((section,), 0)
    from_line(2)
    tails(others, 1)
    from_twin(aside, 0)
    from_beside(1)
    from_twin((section,), 1)
    from_twin((across,), 0)
    from_line(3)
    tails(others, 2)
    from_across(1)
    from_twin((section,), 2)
    from_twin(aside, 1)
    from_beside(2)
    tails(others, 3)
    from_twin((across,), 1)
    from_twin((section,), 3)
    from_across(2)
    from_twin(aside, 2)
    from_beside(3)
    from_twin((across,), 2)
    from_twin(aside, 3)
    from_across(3)
    from_twin((across,), 3)

    for read in reads[6:]:
        read.wait()
    logits = jnp.transpose(total[...])
    slots = lax.broadcasted_iota(jnp.int32, tiles_ref.shape, 0)
    live = slots < count_ref[...]
    own_tiles = columns // TILE
    hits = []
    for n in range(own_tiles):
        match = live & (tiles_ref[...] == device * own_tiles + n)
        hits.append(jnp.max(match.astype(jnp.int32), axis=0, keepdims=True) > 0)
    blocks = [logits[n * TILE:(n + 1) * TILE, :] for n in range(own_tiles)]
    largest = jnp.full(count_ref.shape, LOWEST, jnp.float32)
    for hit, block in zip(hits, blocks):
        largest = jnp.maximum(largest, jnp.where(hit, jnp.max(block, axis=0, keepdims=True), LOWEST))
    terms = jnp.zeros_like(largest)
    for hit, block in zip(hits, blocks):
        terms += jnp.where(hit, jnp.sum(jnp.exp(block - largest), axis=0, keepdims=True), 0.0)
    place = lax.broadcasted_iota(jnp.int32, logits.shape, 0)
    chosen = jnp.sum(jnp.where(place == token_ref[...] - device * columns, logits, 0.0), axis=0, keepdims=True)

    def packed(largest, terms, chosen):
        line = lax.broadcasted_iota(jnp.int32, (8, largest.shape[1]), 0)
        return jnp.where(line == 0, largest, jnp.where(line == 1, terms, jnp.where(line == 2, chosen, 0.0)))

    def combined(stats):
        values = [stats[n] for n in range(stats.shape[0])]
        largest = functools.reduce(jnp.maximum, [value[0:1, :] for value in values])
        terms = sum(value[1:2, :] * jnp.exp(value[0:1, :] - largest) for value in values)
        chosen = sum(value[2:3, :] for value in values)
        return largest, terms, chosen

    slot = section * 2 + core
    plane_stats[pl.ds(slot, 1)] = packed(largest, terms, chosen)[None]
    for peer in plane:
        push(plane_stats.at[slot], plane_stats.at[slot], plane_sems.at[slot], peer)
    for peer_section, peer_tensor in plane:
        peer_slot = peer_section * 2 + peer_tensor % 2
        arrived(plane_stats.at[peer_slot], plane_sems.at[peer_slot])
    line_stats[pl.ds(z, 1)] = packed(*combined(plane_stats))[None]
    for k in range(1, 4):
        push(line_stats.at[z], line_stats.at[z], line_stat_sems.at[z], (section, ((z + k) % 4) * 2 + core))
    for k in range(1, 4):
        peer_z = (z + k) % 4
        arrived(line_stats.at[peer_z], line_stat_sems.at[peer_z])
    largest, terms, chosen = combined(line_stats)
    normalizer = largest + jnp.log(terms)
    normalizer_ref[...] = normalizer
    log_prob_ref[...] = chosen - normalizer

    arrived(next_hbm, next_sem)
    for copy in unconditional:
        copy.wait_send()
    for when, copy in conditional:
        pl.when(when)(copy.wait_send)


def block_shards(
    hidden,
    norm_gain,
    head_weight,
    tile_list,
    tile_count,
    chosen_token,
    chosen_embed,
    stack_state,
    state_table,
):
    height, width = hidden.shape
    row_count = tile_count.shape[0]
    dma = pltpu.SemaphoreType.DMA
    log_prob, normalizer, next_input = pl.pallas_call(
        head_kernel,
        out_shape=(
            jax.ShapeDtypeStruct((1, row_count), jnp.float32),
            jax.ShapeDtypeStruct((1, row_count), jnp.float32),
            jax.ShapeDtypeStruct(chosen_embed.shape, jnp.bfloat16),
        ),
        in_specs=[HBM] * 9,
        out_specs=(VMEM, VMEM, HBM),
        scratch_shapes=[
            pltpu.VMEM((32, height, width), jnp.bfloat16),
            pltpu.VMEM(head_weight.shape, jnp.bfloat16),
            pltpu.VMEM((row_count, head_weight.shape[1]), jnp.float32),
            pltpu.VMEM(hidden.shape, jnp.bfloat16),
            pltpu.VMEM(chosen_embed.shape, jnp.bfloat16),
            pltpu.VMEM(state_table.shape, jnp.bfloat16),
            pltpu.VMEM(chosen_embed.shape, jnp.bfloat16),
            pltpu.VMEM((1, width), jnp.float32),
            pltpu.VMEM(tile_list.shape[::-1], jnp.int32),
            pltpu.VMEM((1, row_count), jnp.int32),
            pltpu.VMEM((1, row_count), jnp.int32),
            pltpu.VMEM((1, height), jnp.int32),
            pltpu.VMEM((8, 8, height), jnp.float32),
            pltpu.VMEM((8, 8, row_count), jnp.float32),
            pltpu.VMEM((4, 8, row_count), jnp.float32),
            dma((80,)),
            dma((32,)),
            dma((32, 3)),
            dma,
            dma((8,)),
            dma((8,)),
            dma((4,)),
            dma((9,)),
        ],
        compiler_params=pltpu.CompilerParams(
            collective_id=0, has_side_effects=True, vmem_limit_bytes=60 * 1024 * 1024
        ),
        name="masked_head",
    )(
        hidden,
        norm_gain[None, :],
        head_weight,
        tile_list.T,
        tile_count[None, :],
        chosen_token[None, :],
        chosen_embed,
        stack_state[None, :],
        state_table,
    )
    return (log_prob[0], normalizer[0], next_input)


def solution(mesh):
    placed = (
        P("section", "tensor"),
        P("tensor"),
        P(None, ("section", "tensor")),
        P(),
        P(),
        P(),
        P("section", "tensor"),
        P("section"),
        P(None, "tensor"),
    )
    small = mesh.shape["section"] == 4 and mesh.shape["tensor"] == 8
    return jax.shard_map(
        block_shards if small else shards,
        mesh=mesh,
        in_specs=placed,
        out_specs=(P(), P(), P("section", "tensor")),
        check_vma=False,
    )
```

```python
import functools

import jax
import jax.numpy as jnp
from jax import lax
from jax.experimental import pallas as pl
from jax.experimental.pallas import tpu as pltpu
from jax.sharding import PartitionSpec as P

D = 16384
TILE = 128
TILES_DEV = 2


EPSILON = 1e-05
NEG_FILL = -1e30


def shifted_2(value, axis, steps):
    count = lax.axis_size(axis)
    pairs = [(source, (source + steps) % count) for source in range(count)]
    return lax.ppermute(value, axis, pairs)


def scale_rows(widened, squares_total, width, gain):
    factor = lax.rsqrt(squares_total / width + EPSILON)
    return (widened * factor[:, None] * gain[None, :]).astype(jnp.bfloat16)


def shards(
    hidden,
    norm_gain,
    head_weight,
    tile_list,
    tile_count,
    chosen_token,
    chosen_embed,
    stack_state,
    state_table,
):
    states = jnp.arange(state_table.shape[0], dtype=jnp.int32)
    one_hot = (stack_state[:, None] == states[None, :]).astype(jnp.bfloat16)
    state_rows = jnp.dot(one_hot, state_table, preferred_element_type=jnp.float32)
    merged = (chosen_embed.astype(jnp.float32) + state_rows).astype(jnp.bfloat16)
    next_input = shifted_2(merged, "section", 1)
    widened = hidden.astype(jnp.float32)
    squares_total = lax.psum(jnp.sum(widened * widened, axis=1), "tensor")
    normed = scale_rows(widened, squares_total, D, norm_gain)
    all_rows = lax.all_gather(normed, "section", axis=0, tiled=True)
    logits = jnp.dot(
        lax.all_gather(all_rows, "tensor", axis=1, tiled=True),
        head_weight,
        preferred_element_type=jnp.float32,
    )
    row_count = logits.shape[0]
    vocab_here = logits.shape[1]
    device = lax.axis_index("section") * lax.axis_size("tensor") + lax.axis_index("tensor")
    own_tiles = device * TILES_DEV + jnp.arange(TILES_DEV, dtype=jnp.int32)
    live_slot = jnp.arange(tile_list.shape[1], dtype=jnp.int32)[None, :] < tile_count[:, None]
    matches = (tile_list[:, :, None] == own_tiles[None, None, :]) & live_slot[:, :, None]
    allowed = jnp.any(matches, axis=1)
    blocks = logits.reshape(row_count, TILES_DEV, TILE)
    allowed_mask = jnp.broadcast_to(allowed[:, :, None], blocks.shape)
    local_top = jnp.max(jnp.where(allowed_mask, blocks, NEG_FILL), axis=(1, 2))
    column = chosen_token - device * vocab_here
    columns = jnp.arange(vocab_here, dtype=jnp.int32)
    picked = jnp.sum(jnp.where(columns[None, :] == column[:, None], logits, 0.0), axis=1)
    row_top = lax.pmax(local_top, ("section", "tensor"))
    shifted = jnp.where(allowed_mask, blocks - row_top[:, None, None], NEG_FILL)
    terms = jnp.sum(jnp.exp(shifted), axis=(1, 2))
    totals, chosen_logit = lax.psum((terms, picked), ("section", "tensor"))
    normalizer = row_top + jnp.log(totals)
    log_prob = chosen_logit - normalizer
    return (log_prob, normalizer, next_input)


LOWEST = -3e38
MESH = pl.DeviceIdType.MESH
HBM = pl.BlockSpec(memory_space=pltpu.HBM)
ANY = pl.BlockSpec(memory_space=pl.ANY)
VMEM = pl.BlockSpec(memory_space=pltpu.VMEM)


def head_kernel(
    hidden_hbm,
    gain_hbm,
    weight_hbm,
    tiles_hbm,
    count_hbm,
    token_hbm,
    embed_hbm,
    state_hbm,
    table_hbm,
    log_prob_ref,
    normalizer_ref,
    next_hbm,
    rows_all,
    weight,
    twin_weight,
    total,
    twin_total,
    from_twin,
    hidden,
    embed,
    table,
    merged,
    gain_ref,
    tiles_ref,
    count_ref,
    token_ref,
    state_ref,
    parts,
    plane_stats,
    line_stats,
    send_sems,
    line_sems,
    recv_sems,
    weight_sems,
    total_sems,
    next_sem,
    parts_sems,
    plane_sems,
    line_stat_sems,
    local_sems,
):
    section = lax.axis_index("section")
    tensor = lax.axis_index("tensor")
    sections = 4
    tensors = 8
    x, y = section % 2, section // 2
    z, core = tensor // 2, tensor % 2
    beside_x = section + 1 - 2 * x
    beside_y = section + 2 - 4 * y
    across = 3 - section
    twin = tensor + 1 - 2 * core
    height, width = hidden.shape
    columns = weight.shape[2]
    device = section * tensors + tensor

    reads = [
        pltpu.make_async_copy(source, target, local_sems.at[n])
        for n, (source, target) in enumerate(
            (
                (hidden_hbm, hidden),
                (table_hbm, table),
                (embed_hbm, embed),
                (state_hbm, state_ref),
                (gain_hbm, gain_ref),
                (tiles_hbm, tiles_ref),
                (count_hbm, count_ref),
                (token_hbm, token_ref),
            )
        )
    ]
    upper = z // 2
    order = []
    mirrored = z + upper * (3 - 2 * z)
    for place in (mirrored, 1 - mirrored, 2, 3):
        order.append(place + upper * (3 - 2 * place))

    def features(place, of_core):
        return pl.ds(pl.multiple_of((place * 2 + of_core) * width, width), width)

    for read in reads:
        read.start()
    weight_reads = [
        pltpu.make_async_copy(weight_hbm.at[features(place, core)], weight.at[place], local_sems.at[len(reads) + n])
        for n, place in enumerate(order)
    ]
    for read in weight_reads:
        read.start()

    plane = [((section + k // 2) % sections, (tensor // 2) * 2 + (core + k) % 2) for k in range(1, 8)]
    line = [(section, (tensor + k) % tensors) for k in range(1, 8)]
    barrier = pltpu.get_barrier_semaphore()
    greeted = plane + [(section, ((z + k) % 4) * 2 + c) for k in range(1, 4) for c in range(2)]
    for peer in greeted:
        pl.semaphore_signal(barrier, inc=1, device_id=peer, device_id_type=MESH)

    reads[0].wait()
    widened = hidden[...].astype(jnp.float32)
    squares = jnp.sum(widened * widened, axis=1, keepdims=True)
    laid = jnp.transpose(jnp.broadcast_to(squares, (height, 128)))[0:8, :]
    parts[pl.ds(tensor, 1)] = laid[None]
    pl.semaphore_wait(barrier, len(greeted))

    unconditional = []
    conditional = []

    def push(source, target, receive, peer, when=None):
        if when is None:
            copy = pltpu.make_async_remote_copy(
                src_ref=source,
                dst_ref=target,
                send_sem=send_sems.at[len(unconditional)],
                recv_sem=receive,
                device_id=peer,
                device_id_type=MESH,
            )
            unconditional.append(copy)
            copy.start()
        else:
            copy = pltpu.make_async_remote_copy(
                src_ref=source,
                dst_ref=target,
                send_sem=line_sems.at[len(conditional)],
                recv_sem=receive,
                device_id=peer,
                device_id_type=MESH,
            )
            conditional.append((when, copy))
            pl.when(when)(copy.start)

    def arrived(target, receive):
        pltpu.make_async_remote_copy(
            src_ref=target,
            dst_ref=target,
            send_sem=send_sems.at[0],
            recv_sem=receive,
            device_id=(section, twin),
            device_id_type=MESH,
        ).wait_recv()

    def send_weight(step):
        place = order[step]
        source = weight_hbm.at[features(place, 1 - core)]
        push(source, twin_weight.at[place], weight_sems.at[place], (section, twin))

    for peer in line:
        push(parts.at[tensor], parts.at[tensor], parts_sems.at[tensor], peer)

    reads[3].wait()
    states = lax.broadcasted_iota(jnp.int32, (table.shape[0], height), 0)
    one_hot = jnp.transpose((states == state_ref[...]).astype(jnp.float32)).astype(jnp.bfloat16)
    reads[1].wait()
    reads[2].wait()
    state_rows = jnp.dot(one_hot, table[...], preferred_element_type=jnp.float32)
    merged[...] = (embed[...].astype(jnp.float32) + state_rows).astype(jnp.bfloat16)
    push(merged, next_hbm, next_sem, ((section + 1) % sections, tensor))

    send_weight(0)

    for _, peer in line:
        arrived(parts.at[peer], parts_sems.at[peer])
    squares_total = jnp.sum(parts[...], axis=0)[0:1, :]
    reads[4].wait()
    factor = lax.rsqrt(squares_total / (width * tensors) + EPSILON)
    factor = jnp.transpose(jnp.broadcast_to(factor, (128, height)))[:, 0:1]
    own = section * 4 + z
    rows_all[pl.ds(own, 1)] = (hidden[...].astype(jnp.float32) * factor * gain_ref[...]).astype(jnp.bfloat16)[None]

    first = height * 3 // 4
    tail = pl.ds(first, height - first)

    def halves(step):
        size = (first if step else height) // 2
        return pl.ds(0, size), pl.ds(size, size)

    def multiply(source, step):
        place = order[step]
        row = pl.ds(pl.multiple_of(source * height, height), height)
        block = rows_all[source * 4 + place]
        for sums, by in ((twin_total, twin_weight), (total, weight)):
            product = jnp.dot(block, by[place], preferred_element_type=jnp.float32)
            if step:
                product += sums[row, :]
            sums[row, :] = product
        if step == 3:
            push(twin_total.at[row], from_twin.at[row], total_sems.at[source], (section, twin))

    def weights_there(step):
        weight_reads[step].wait()
        arrived(twin_weight.at[order[step]], weight_sems.at[order[step]])

    def along(piece, receive, place):
        push(piece, piece, receive, (section, tensor + 2), (place <= z) & (z < 3))
        push(piece, piece, receive, (section, tensor - 2), (place >= z) & (z > 0))

    def from_line(step):
        place = order[step]
        block = section * 4 + place
        whole = rows_all.at[block]
        if step:
            arrived(whole, recv_sems.at[block, 0])
        along(whole, recv_sems.at[block, 0], place)
        for peer, parts_in_order in ((beside_x, (0, 1)), (beside_y, (1, 0))):
            for part in parts_in_order:
                piece = rows_all.at[block, halves(step)[part]]
                push(piece, piece, recv_sems.at[block, part], (peer, tensor))
        if step == 0:
            for later in range(1, 4):
                send_weight(later)
        weights_there(step)
        multiply(section, step)

    def tails(sources, step):
        for source in sources:
            block = source * 4 + order[step]
            piece = rows_all.at[block, tail]
            if step:
                arrived(piece, recv_sems.at[block, 2])
            along(piece, recv_sems.at[block, 2], order[step])

    def from_beside(step):
        for source, onward, part in ((beside_x, beside_y, 0), (beside_y, beside_x, 1)):
            block = source * 4 + order[step]
            piece = rows_all.at[block, halves(step)[part]]
            arrived(piece, recv_sems.at[block, part])
            push(piece, piece, recv_sems.at[block, part], (onward, tensor))
        for source, part in ((beside_x, 1), (beside_y, 0)):
            block = source * 4 + order[step]
            piece = rows_all.at[block, halves(step)[part]]
            arrived(piece, recv_sems.at[block, part])
            if step == 0:
                tails((source,), 0)
        multiply(beside_x, step)
        multiply(beside_y, step)

    def from_across(step):
        block = across * 4 + order[step]
        for part in range(2):
            arrived(rows_all.at[block, halves(step)[part]], recv_sems.at[block, part])
        if step == 0:
            tails((across,), 0)
        multiply(across, step)

    others = (beside_x, beside_y, across)
    from_line(0)
    from_beside(0)
    from_line(1)
    from_across(0)
    from_line(2)
    tails(others, 1)
    from_beside(1)
    from_line(3)
    tails(others, 2)
    from_across(1)
    from_beside(2)
    tails(others, 3)
    from_across(2)
    from_beside(3)
    from_across(3)

    for read in reads[5:]:
        read.wait()
    for source in (section, *others):
        row = pl.ds(pl.multiple_of(source * height, height), height)
        arrived(from_twin.at[row], total_sems.at[source])
    logits = jnp.transpose(total[...] + from_twin[...])
    slots = lax.broadcasted_iota(jnp.int32, tiles_ref.shape, 0)
    live = slots < count_ref[...]
    own_tiles = columns // TILE
    hits = []
    for n in range(own_tiles):
        match = live & (tiles_ref[...] == device * own_tiles + n)
        hits.append(jnp.max(match.astype(jnp.int32), axis=0, keepdims=True) > 0)
    blocks = [logits[n * TILE:(n + 1) * TILE, :] for n in range(own_tiles)]
    largest = jnp.full(count_ref.shape, LOWEST, jnp.float32)
    for hit, block in zip(hits, blocks):
        largest = jnp.maximum(largest, jnp.where(hit, jnp.max(block, axis=0, keepdims=True), LOWEST))
    terms = jnp.zeros_like(largest)
    for hit, block in zip(hits, blocks):
        terms += jnp.where(hit, jnp.sum(jnp.exp(block - largest), axis=0, keepdims=True), 0.0)
    place = lax.broadcasted_iota(jnp.int32, logits.shape, 0)
    chosen = jnp.sum(jnp.where(place == token_ref[...] - device * columns, logits, 0.0), axis=0, keepdims=True)

    def packed(largest, terms, chosen):
        line = lax.broadcasted_iota(jnp.int32, (8, largest.shape[1]), 0)
        return jnp.where(line == 0, largest, jnp.where(line == 1, terms, jnp.where(line == 2, chosen, 0.0)))

    def combined(stats):
        values = [stats[n] for n in range(stats.shape[0])]
        largest = functools.reduce(jnp.maximum, [value[0:1, :] for value in values])
        terms = sum(value[1:2, :] * jnp.exp(value[0:1, :] - largest) for value in values)
        chosen = sum(value[2:3, :] for value in values)
        return largest, terms, chosen

    slot = section * 2 + core
    plane_stats[pl.ds(slot, 1)] = packed(largest, terms, chosen)[None]
    for peer in plane:
        push(plane_stats.at[slot], plane_stats.at[slot], plane_sems.at[slot], peer)
    for peer_section, peer_tensor in plane:
        peer_slot = peer_section * 2 + peer_tensor % 2
        arrived(plane_stats.at[peer_slot], plane_sems.at[peer_slot])
    line_stats[pl.ds(z, 1)] = packed(*combined(plane_stats))[None]
    for k in range(1, 4):
        push(line_stats.at[z], line_stats.at[z], line_stat_sems.at[z], (section, ((z + k) % 4) * 2 + core))
    for k in range(1, 4):
        peer_z = (z + k) % 4
        arrived(line_stats.at[peer_z], line_stat_sems.at[peer_z])
    largest, terms, chosen = combined(line_stats)
    normalizer = largest + jnp.log(terms)
    normalizer_ref[...] = normalizer
    log_prob_ref[...] = chosen - normalizer

    arrived(next_hbm, next_sem)
    for copy in unconditional:
        copy.wait_send()
    for when, copy in conditional:
        pl.when(when)(copy.wait_send)


def block_shards(
    hidden,
    norm_gain,
    head_weight,
    tile_list,
    tile_count,
    chosen_token,
    chosen_embed,
    stack_state,
    state_table,
):
    height, width = hidden.shape
    row_count = tile_count.shape[0]
    columns = head_weight.shape[1]
    dma = pltpu.SemaphoreType.DMA
    log_prob, normalizer, next_input = pl.pallas_call(
        head_kernel,
        out_shape=(
            jax.ShapeDtypeStruct((1, row_count), jnp.float32),
            jax.ShapeDtypeStruct((1, row_count), jnp.float32),
            jax.ShapeDtypeStruct(chosen_embed.shape, jnp.bfloat16),
        ),
        in_specs=[HBM] * 9,
        out_specs=(VMEM, VMEM, ANY),
        scratch_shapes=[
            pltpu.VMEM((16, height, width), jnp.bfloat16),
            pltpu.VMEM((4, width, columns), jnp.bfloat16),
            pltpu.VMEM((4, width, columns), jnp.bfloat16),
            pltpu.VMEM((row_count, columns), jnp.float32),
            pltpu.VMEM((row_count, columns), jnp.float32),
            pltpu.VMEM((row_count, columns), jnp.float32),
            pltpu.VMEM(hidden.shape, jnp.bfloat16),
            pltpu.VMEM(chosen_embed.shape, jnp.bfloat16),
            pltpu.VMEM(state_table.shape, jnp.bfloat16),
            pltpu.VMEM(chosen_embed.shape, jnp.bfloat16),
            pltpu.VMEM((1, width), jnp.float32),
            pltpu.VMEM(tile_list.shape[::-1], jnp.int32),
            pltpu.VMEM((1, row_count), jnp.int32),
            pltpu.VMEM((1, row_count), jnp.int32),
            pltpu.VMEM((1, height), jnp.int32),
            pltpu.VMEM((8, 8, height), jnp.float32),
            pltpu.VMEM((8, 8, row_count), jnp.float32),
            pltpu.VMEM((4, 8, row_count), jnp.float32),
            dma((80,)),
            dma((32,)),
            dma((16, 3)),
            dma((4,)),
            dma((4,)),
            dma,
            dma((8,)),
            dma((8,)),
            dma((4,)),
            dma((12,)),
        ],
        compiler_params=pltpu.CompilerParams(
            collective_id=0, has_side_effects=True, vmem_limit_bytes=60 * 1024 * 1024
        ),
        name="masked_head",
    )(
        hidden,
        norm_gain[None, :],
        head_weight,
        tile_list.T,
        tile_count[None, :],
        chosen_token[None, :],
        chosen_embed,
        stack_state[None, :],
        state_table,
    )
    return (log_prob[0], normalizer[0], next_input)


def solution(mesh):
    placed = (
        P("section", "tensor"),
        P("tensor"),
        P(None, ("section", "tensor")),
        P(),
        P(),
        P(),
        P("section", "tensor"),
        P("section"),
        P(None, "tensor"),
    )
    small = mesh.shape["section"] == 4 and mesh.shape["tensor"] == 8
    return jax.shard_map(
        block_shards if small else shards,
        mesh=mesh,
        in_specs=placed,
        out_specs=(P(), P(), P("section", "tensor")),
        check_vma=False,
    )
```

```python
import functools

import jax
import jax.numpy as jnp
from jax import lax
from jax.experimental import pallas as pl
from jax.experimental.pallas import tpu as pltpu
from jax.sharding import PartitionSpec as P

D = 16384
TILE = 128
TILES_DEV = 2


EPSILON = 1e-05
NEG_FILL = -1e30


def shifted_2(value, axis, steps):
    count = lax.axis_size(axis)
    pairs = [(source, (source + steps) % count) for source in range(count)]
    return lax.ppermute(value, axis, pairs)


def scale_rows(widened, squares_total, width, gain):
    factor = lax.rsqrt(squares_total / width + EPSILON)
    return (widened * factor[:, None] * gain[None, :]).astype(jnp.bfloat16)


def shards(
    hidden,
    norm_gain,
    head_weight,
    tile_list,
    tile_count,
    chosen_token,
    chosen_embed,
    stack_state,
    state_table,
):
    states = jnp.arange(state_table.shape[0], dtype=jnp.int32)
    one_hot = (stack_state[:, None] == states[None, :]).astype(jnp.bfloat16)
    state_rows = jnp.dot(one_hot, state_table, preferred_element_type=jnp.float32)
    merged = (chosen_embed.astype(jnp.float32) + state_rows).astype(jnp.bfloat16)
    next_input = shifted_2(merged, "section", 1)
    widened = hidden.astype(jnp.float32)
    squares_total = lax.psum(jnp.sum(widened * widened, axis=1), "tensor")
    normed = scale_rows(widened, squares_total, D, norm_gain)
    all_rows = lax.all_gather(normed, "section", axis=0, tiled=True)
    logits = jnp.dot(
        lax.all_gather(all_rows, "tensor", axis=1, tiled=True),
        head_weight,
        preferred_element_type=jnp.float32,
    )
    row_count = logits.shape[0]
    vocab_here = logits.shape[1]
    device = lax.axis_index("section") * lax.axis_size("tensor") + lax.axis_index("tensor")
    own_tiles = device * TILES_DEV + jnp.arange(TILES_DEV, dtype=jnp.int32)
    live_slot = jnp.arange(tile_list.shape[1], dtype=jnp.int32)[None, :] < tile_count[:, None]
    matches = (tile_list[:, :, None] == own_tiles[None, None, :]) & live_slot[:, :, None]
    allowed = jnp.any(matches, axis=1)
    blocks = logits.reshape(row_count, TILES_DEV, TILE)
    allowed_mask = jnp.broadcast_to(allowed[:, :, None], blocks.shape)
    local_top = jnp.max(jnp.where(allowed_mask, blocks, NEG_FILL), axis=(1, 2))
    column = chosen_token - device * vocab_here
    columns = jnp.arange(vocab_here, dtype=jnp.int32)
    picked = jnp.sum(jnp.where(columns[None, :] == column[:, None], logits, 0.0), axis=1)
    row_top = lax.pmax(local_top, ("section", "tensor"))
    shifted = jnp.where(allowed_mask, blocks - row_top[:, None, None], NEG_FILL)
    terms = jnp.sum(jnp.exp(shifted), axis=(1, 2))
    totals, chosen_logit = lax.psum((terms, picked), ("section", "tensor"))
    normalizer = row_top + jnp.log(totals)
    log_prob = chosen_logit - normalizer
    return (log_prob, normalizer, next_input)


LOWEST = -3e38
MESH = pl.DeviceIdType.MESH
HBM = pl.BlockSpec(memory_space=pltpu.HBM)
ANY = pl.BlockSpec(memory_space=pl.ANY)
VMEM = pl.BlockSpec(memory_space=pltpu.VMEM)


def head_kernel(
    hidden_hbm,
    gain_hbm,
    weight_hbm,
    tiles_hbm,
    count_hbm,
    token_hbm,
    embed_hbm,
    state_hbm,
    table_hbm,
    stats_ref,
    next_hbm,
    rows_all,
    weight,
    twin_weight,
    total,
    twin_total,
    from_twin,
    hidden,
    embed,
    table,
    merged,
    gain_ref,
    tiles_ref,
    count_ref,
    token_ref,
    state_ref,
    parts,
    plane_stats,
    line_stats,
    send_sems,
    line_sems,
    recv_sems,
    weight_sems,
    total_sems,
    next_sem,
    parts_sems,
    plane_sems,
    line_stat_sems,
    local_sems,
):
    section = lax.axis_index("section")
    tensor = lax.axis_index("tensor")
    sections = 4
    tensors = 8
    x, y = section % 2, section // 2
    z, core = tensor // 2, tensor % 2
    beside_x = section + 1 - 2 * x
    beside_y = section + 2 - 4 * y
    across = 3 - section
    twin = tensor + 1 - 2 * core
    height, width = hidden.shape
    columns = weight.shape[2]
    device = section * tensors + tensor

    reads = [
        pltpu.make_async_copy(source, target, local_sems.at[n])
        for n, (source, target) in enumerate(
            (
                (hidden_hbm, hidden),
                (table_hbm, table),
                (embed_hbm, embed),
                (state_hbm, state_ref),
                (gain_hbm, gain_ref),
                (tiles_hbm, tiles_ref),
                (count_hbm, count_ref),
                (token_hbm, token_ref),
            )
        )
    ]
    upper = z // 2
    order = []
    mirrored = z + upper * (3 - 2 * z)
    for place in (mirrored, 1 - mirrored, 2, 3):
        order.append(place + upper * (3 - 2 * place))

    def features(place, of_core):
        return pl.ds(pl.multiple_of((place * 2 + of_core) * width, width), width)

    for read in reads:
        read.start()
    weight_reads = [
        pltpu.make_async_copy(weight_hbm.at[features(place, core)], weight.at[place], local_sems.at[len(reads) + n])
        for n, place in enumerate(order)
    ]
    for read in weight_reads:
        read.start()

    plane = [((section + k // 2) % sections, (tensor // 2) * 2 + (core + k) % 2) for k in range(1, 8)]
    line = [(section, (tensor + k) % tensors) for k in range(1, 8)]
    barrier = pltpu.get_barrier_semaphore()
    greeted = plane + [(section, ((z + k) % 4) * 2 + c) for k in range(1, 4) for c in range(2)]
    for peer in greeted:
        pl.semaphore_signal(barrier, inc=1, device_id=peer, device_id_type=MESH)

    reads[0].wait()
    widened = hidden[...].astype(jnp.float32)
    squares = jnp.sum(widened * widened, axis=1, keepdims=True)
    laid = jnp.transpose(jnp.broadcast_to(squares, (height, 128)))[0:8, :]
    parts[pl.ds(tensor, 1)] = laid[None]
    pl.semaphore_wait(barrier, len(greeted))

    unconditional = []
    conditional = []

    def push(source, target, receive, peer, when=None):
        if when is None:
            copy = pltpu.make_async_remote_copy(
                src_ref=source,
                dst_ref=target,
                send_sem=send_sems.at[len(unconditional)],
                recv_sem=receive,
                device_id=peer,
                device_id_type=MESH,
            )
            unconditional.append(copy)
            copy.start()
        else:
            copy = pltpu.make_async_remote_copy(
                src_ref=source,
                dst_ref=target,
                send_sem=line_sems.at[len(conditional)],
                recv_sem=receive,
                device_id=peer,
                device_id_type=MESH,
            )
            conditional.append((when, copy))
            pl.when(when)(copy.start)

    def arrived(target, receive):
        pltpu.make_async_remote_copy(
            src_ref=target,
            dst_ref=target,
            send_sem=send_sems.at[0],
            recv_sem=receive,
            device_id=(section, twin),
            device_id_type=MESH,
        ).wait_recv()

    def send_weight(step):
        place = order[step]
        source = weight_hbm.at[features(place, 1 - core)]
        push(source, twin_weight.at[place], weight_sems.at[place], (section, twin))

    for peer in line:
        push(parts.at[tensor], parts.at[tensor], parts_sems.at[tensor], peer)

    reads[3].wait()
    states = lax.broadcasted_iota(jnp.int32, (table.shape[0], height), 0)
    one_hot = jnp.transpose((states == state_ref[...]).astype(jnp.float32)).astype(jnp.bfloat16)
    reads[1].wait()
    reads[2].wait()
    state_rows = jnp.dot(one_hot, table[...], preferred_element_type=jnp.float32)
    merged[...] = (embed[...].astype(jnp.float32) + state_rows).astype(jnp.bfloat16)
    push(merged, next_hbm, next_sem, ((section + 1) % sections, tensor))

    send_weight(0)

    for _, peer in line:
        arrived(parts.at[peer], parts_sems.at[peer])
    squares_total = jnp.sum(parts[...], axis=0)[0:1, :]
    reads[4].wait()
    factor = lax.rsqrt(squares_total / (width * tensors) + EPSILON)
    factor = jnp.transpose(jnp.broadcast_to(factor, (128, height)))[:, 0:1]
    own = section * 4 + z
    rows_all[pl.ds(own, 1)] = (hidden[...].astype(jnp.float32) * factor * gain_ref[...]).astype(jnp.bfloat16)[None]

    first = height * 3 // 4
    tail = pl.ds(first, height - first)

    def halves(step):
        size = (first if step else height) // 2
        return pl.ds(0, size), pl.ds(size, size)

    def multiply(source, step):
        place = order[step]
        row = pl.ds(pl.multiple_of(source * height, height), height)
        block = rows_all[source * 4 + place]
        for sums, by in ((twin_total, twin_weight), (total, weight)):
            product = jnp.dot(block, by[place], preferred_element_type=jnp.float32)
            if step:
                product += sums[row, :]
            sums[row, :] = product
        if step == 3:
            push(twin_total.at[row], from_twin.at[row], total_sems.at[source], (section, twin))

    def weights_there(step):
        weight_reads[step].wait()
        arrived(twin_weight.at[order[step]], weight_sems.at[order[step]])

    def along(piece, receive, place):
        push(piece, piece, receive, (section, tensor + 2), (place <= z) & (z < 3))
        push(piece, piece, receive, (section, tensor - 2), (place >= z) & (z > 0))

    middle, outer = mirrored == 1, mirrored == 0

    def whole_there(step, when=None):
        block = section * 4 + order[step]
        wait = functools.partial(arrived, rows_all.at[block], recv_sems.at[block, 0])
        if when is None:
            wait()
        else:
            pl.when(when)(wait)

    def pass_whole(step):
        block = section * 4 + order[step]
        along(rows_all.at[block], recv_sems.at[block, 0], order[step])

    def from_line(step):
        block = section * 4 + order[step]
        for peer, parts_in_order in ((beside_x, (0, 1)), (beside_y, (1, 0))):
            for part in parts_in_order:
                piece = rows_all.at[block, halves(step)[part]]
                push(piece, piece, recv_sems.at[block, part], (peer, tensor))
        if step == 0:
            for later in range(1, 4):
                send_weight(later)
        weights_there(step)
        multiply(section, step)

    def tails(sources, step, when=None):
        for source in sources:
            block = source * 4 + order[step]
            piece = rows_all.at[block, tail]
            if step:
                wait = functools.partial(arrived, piece, recv_sems.at[block, 2])
                if when is None:
                    wait()
                else:
                    pl.when(when)(wait)
            if when is not outer:
                along(piece, recv_sems.at[block, 2], order[step])

    def from_beside(step):
        for source, onward, part in ((beside_x, beside_y, 0), (beside_y, beside_x, 1)):
            block = source * 4 + order[step]
            piece = rows_all.at[block, halves(step)[part]]
            arrived(piece, recv_sems.at[block, part])
            push(piece, piece, recv_sems.at[block, part], (onward, tensor))
        for source, part in ((beside_x, 1), (beside_y, 0)):
            block = source * 4 + order[step]
            piece = rows_all.at[block, halves(step)[part]]
            arrived(piece, recv_sems.at[block, part])
            if step == 0:
                tails((source,), 0)
        multiply(beside_x, step)
        multiply(beside_y, step)

    def from_across(step):
        block = across * 4 + order[step]
        for part in range(2):
            arrived(rows_all.at[block, halves(step)[part]], recv_sems.at[block, part])
        if step == 0:
            tails((across,), 0)
        multiply(across, step)

    others = (beside_x, beside_y, across)
    pass_whole(0)
    from_line(0)
    whole_there(1)
    pass_whole(1)
    from_line(1)
    whole_there(2, middle)
    pass_whole(2)
    from_beside(0)
    whole_there(2, outer)
    from_line(2)
    from_across(0)
    whole_there(3, middle)
    pass_whole(3)
    tails(others, 1)
    tails(others, 2, middle)
    from_beside(1)
    whole_there(3, outer)
    from_line(3)
    tails(others, 3, middle)
    from_across(1)
    tails(others, 2, outer)
    from_beside(2)
    tails(others, 3, outer)
    from_across(2)
    from_beside(3)
    from_across(3)

    for read in reads[5:]:
        read.wait()
    for source in (section, *others):
        row = pl.ds(pl.multiple_of(source * height, height), height)
        arrived(from_twin.at[row], total_sems.at[source])
    logits = jnp.transpose(total[...] + from_twin[...])
    slots = lax.broadcasted_iota(jnp.int32, tiles_ref.shape, 0)
    live = slots < count_ref[...]
    own_tiles = columns // TILE
    hits = []
    for n in range(own_tiles):
        match = live & (tiles_ref[...] == device * own_tiles + n)
        hits.append(jnp.max(match.astype(jnp.int32), axis=0, keepdims=True) > 0)
    blocks = [logits[n * TILE:(n + 1) * TILE, :] for n in range(own_tiles)]
    largest = jnp.full(count_ref.shape, LOWEST, jnp.float32)
    for hit, block in zip(hits, blocks):
        largest = jnp.maximum(largest, jnp.where(hit, jnp.max(block, axis=0, keepdims=True), LOWEST))
    terms = jnp.zeros_like(largest)
    for hit, block in zip(hits, blocks):
        terms += jnp.where(hit, jnp.sum(jnp.exp(block - largest), axis=0, keepdims=True), 0.0)
    place = lax.broadcasted_iota(jnp.int32, logits.shape, 0)
    chosen = jnp.sum(jnp.where(place == token_ref[...] - device * columns, logits, 0.0), axis=0, keepdims=True)

    def packed(largest, terms, chosen):
        line = lax.broadcasted_iota(jnp.int32, (8, largest.shape[1]), 0)
        return jnp.where(line == 0, largest, jnp.where(line == 1, terms, jnp.where(line == 2, chosen, 0.0)))

    def combined(stats):
        values = [stats[n] for n in range(stats.shape[0])]
        largest = functools.reduce(jnp.maximum, [value[0:1, :] for value in values])
        terms = sum(value[1:2, :] * jnp.exp(value[0:1, :] - largest) for value in values)
        chosen = sum(value[2:3, :] for value in values)
        return largest, terms, chosen

    slot = section * 2 + core
    plane_stats[pl.ds(slot, 1)] = packed(largest, terms, chosen)[None]
    for peer in plane:
        push(plane_stats.at[slot], plane_stats.at[slot], plane_sems.at[slot], peer)
    for peer_section, peer_tensor in plane:
        peer_slot = peer_section * 2 + peer_tensor % 2
        arrived(plane_stats.at[peer_slot], plane_sems.at[peer_slot])
    line_stats[pl.ds(z, 1)] = packed(*combined(plane_stats))[None]
    for k in range(1, 4):
        push(line_stats.at[z], line_stats.at[z], line_stat_sems.at[z], (section, ((z + k) % 4) * 2 + core))
    for k in range(1, 4):
        peer_z = (z + k) % 4
        arrived(line_stats.at[peer_z], line_stat_sems.at[peer_z])
    largest, terms, chosen = combined(line_stats)
    stats_ref[...] = packed(largest + jnp.log(terms), chosen, chosen)

    arrived(next_hbm, next_sem)
    for copy in unconditional:
        copy.wait_send()
    for when, copy in conditional:
        pl.when(when)(copy.wait_send)


def block_shards(
    hidden,
    norm_gain,
    head_weight,
    tile_list,
    tile_count,
    chosen_token,
    chosen_embed,
    stack_state,
    state_table,
):
    height, width = hidden.shape
    row_count = tile_count.shape[0]
    columns = head_weight.shape[1]
    dma = pltpu.SemaphoreType.DMA
    stats, next_input = pl.pallas_call(
        head_kernel,
        out_shape=(
            jax.ShapeDtypeStruct((8, row_count), jnp.float32),
            jax.ShapeDtypeStruct(chosen_embed.shape, jnp.bfloat16),
        ),
        in_specs=[HBM] * 9,
        out_specs=(VMEM, ANY),
        scratch_shapes=[
            pltpu.VMEM((16, height, width), jnp.bfloat16),
            pltpu.VMEM((4, width, columns), jnp.bfloat16),
            pltpu.VMEM((4, width, columns), jnp.bfloat16),
            pltpu.VMEM((row_count, columns), jnp.float32),
            pltpu.VMEM((row_count, columns), jnp.float32),
            pltpu.VMEM((row_count, columns), jnp.float32),
            pltpu.VMEM(hidden.shape, jnp.bfloat16),
            pltpu.VMEM(chosen_embed.shape, jnp.bfloat16),
            pltpu.VMEM(state_table.shape, jnp.bfloat16),
            pltpu.VMEM(chosen_embed.shape, jnp.bfloat16),
            pltpu.VMEM((1, width), jnp.float32),
            pltpu.VMEM(tile_list.shape[::-1], jnp.int32),
            pltpu.VMEM((1, row_count), jnp.int32),
            pltpu.VMEM((1, row_count), jnp.int32),
            pltpu.VMEM((1, height), jnp.int32),
            pltpu.VMEM((8, 8, height), jnp.float32),
            pltpu.VMEM((8, 8, row_count), jnp.float32),
            pltpu.VMEM((4, 8, row_count), jnp.float32),
            dma((80,)),
            dma((32,)),
            dma((16, 3)),
            dma((4,)),
            dma((4,)),
            dma,
            dma((8,)),
            dma((8,)),
            dma((4,)),
            dma((12,)),
        ],
        compiler_params=pltpu.CompilerParams(
            collective_id=0, has_side_effects=True, vmem_limit_bytes=60 * 1024 * 1024
        ),
        name="masked_head",
    )(
        hidden,
        norm_gain[None, :],
        head_weight,
        tile_list.T,
        tile_count[None, :],
        chosen_token[None, :],
        chosen_embed,
        stack_state[None, :],
        state_table,
    )
    return (stats[1] - stats[0], stats[0], next_input)


def solution(mesh):
    placed = (
        P("section", "tensor"),
        P("tensor"),
        P(None, ("section", "tensor")),
        P(),
        P(),
        P(),
        P("section", "tensor"),
        P("section"),
        P(None, "tensor"),
    )
    small = mesh.shape["section"] == 4 and mesh.shape["tensor"] == 8
    return jax.shard_map(
        block_shards if small else shards,
        mesh=mesh,
        in_specs=placed,
        out_specs=(P(), P(), P("section", "tensor")),
        check_vma=False,
    )
```

```python
import functools

import jax
import jax.numpy as jnp
from jax import lax
from jax.experimental import pallas as pl
from jax.experimental.pallas import tpu as pltpu
from jax.sharding import PartitionSpec as P

D = 16384
TILE = 128
TILES_DEV = 2


EPSILON = 1e-05
NEG_FILL = -1e30


def shifted_2(value, axis, steps):
    count = lax.axis_size(axis)
    pairs = [(source, (source + steps) % count) for source in range(count)]
    return lax.ppermute(value, axis, pairs)


def scale_rows(widened, squares_total, width, gain):
    factor = lax.rsqrt(squares_total / width + EPSILON)
    return (widened * factor[:, None] * gain[None, :]).astype(jnp.bfloat16)


def shards(
    hidden,
    norm_gain,
    head_weight,
    tile_list,
    tile_count,
    chosen_token,
    chosen_embed,
    stack_state,
    state_table,
):
    states = jnp.arange(state_table.shape[0], dtype=jnp.int32)
    one_hot = (stack_state[:, None] == states[None, :]).astype(jnp.bfloat16)
    state_rows = jnp.dot(one_hot, state_table, preferred_element_type=jnp.float32)
    merged = (chosen_embed.astype(jnp.float32) + state_rows).astype(jnp.bfloat16)
    next_input = shifted_2(merged, "section", 1)
    widened = hidden.astype(jnp.float32)
    squares_total = lax.psum(jnp.sum(widened * widened, axis=1), "tensor")
    normed = scale_rows(widened, squares_total, D, norm_gain)
    all_rows = lax.all_gather(normed, "section", axis=0, tiled=True)
    logits = jnp.dot(
        lax.all_gather(all_rows, "tensor", axis=1, tiled=True),
        head_weight,
        preferred_element_type=jnp.float32,
    )
    row_count = logits.shape[0]
    vocab_here = logits.shape[1]
    device = lax.axis_index("section") * lax.axis_size("tensor") + lax.axis_index("tensor")
    own_tiles = device * TILES_DEV + jnp.arange(TILES_DEV, dtype=jnp.int32)
    live_slot = jnp.arange(tile_list.shape[1], dtype=jnp.int32)[None, :] < tile_count[:, None]
    matches = (tile_list[:, :, None] == own_tiles[None, None, :]) & live_slot[:, :, None]
    allowed = jnp.any(matches, axis=1)
    blocks = logits.reshape(row_count, TILES_DEV, TILE)
    allowed_mask = jnp.broadcast_to(allowed[:, :, None], blocks.shape)
    local_top = jnp.max(jnp.where(allowed_mask, blocks, NEG_FILL), axis=(1, 2))
    column = chosen_token - device * vocab_here
    columns = jnp.arange(vocab_here, dtype=jnp.int32)
    picked = jnp.sum(jnp.where(columns[None, :] == column[:, None], logits, 0.0), axis=1)
    row_top = lax.pmax(local_top, ("section", "tensor"))
    shifted = jnp.where(allowed_mask, blocks - row_top[:, None, None], NEG_FILL)
    terms = jnp.sum(jnp.exp(shifted), axis=(1, 2))
    totals, chosen_logit = lax.psum((terms, picked), ("section", "tensor"))
    normalizer = row_top + jnp.log(totals)
    log_prob = chosen_logit - normalizer
    return (log_prob, normalizer, next_input)


LOWEST = -3e38
MESH = pl.DeviceIdType.MESH
HBM = pl.BlockSpec(memory_space=pltpu.HBM)
ANY = pl.BlockSpec(memory_space=pl.ANY)
VMEM = pl.BlockSpec(memory_space=pltpu.VMEM)


def head_kernel(
    hidden_hbm,
    gain_hbm,
    weight_hbm,
    tiles_hbm,
    count_hbm,
    token_hbm,
    embed_hbm,
    state_hbm,
    table_hbm,
    stats_ref,
    next_hbm,
    rows_all,
    weight,
    twin_weight,
    total,
    twin_total,
    from_twin,
    embed,
    table,
    merged,
    gains,
    factors,
    tiles_ref,
    count_ref,
    token_ref,
    state_ref,
    parts,
    plane_stats,
    line_stats,
    send_sems,
    line_sems,
    recv_sems,
    weight_sems,
    total_sems,
    gain_sems,
    factor_sems,
    next_sem,
    parts_sems,
    plane_sems,
    line_stat_sems,
    local_sems,
):
    section = lax.axis_index("section")
    tensor = lax.axis_index("tensor")
    sections = 4
    tensors = 8
    x, y = section % 2, section // 2
    z, core = tensor // 2, tensor % 2
    beside_x = section + 1 - 2 * x
    beside_y = section + 2 - 4 * y
    across = 3 - section
    others = (beside_x, beside_y, across)
    twin = tensor + 1 - 2 * core
    height, width = embed.shape
    columns = weight.shape[2]
    device = section * tensors + tensor

    own = section * 4 + z

    reads = [
        pltpu.make_async_copy(source, target, local_sems.at[n])
        for n, (source, target) in enumerate(
            (
                (hidden_hbm, rows_all.at[own]),
                (table_hbm, table),
                (embed_hbm, embed),
                (state_hbm, state_ref),
                (gain_hbm, gains.at[z]),
                (tiles_hbm, tiles_ref),
                (count_hbm, count_ref),
                (token_hbm, token_ref),
            )
        )
    ]
    upper = z // 2
    order = []
    mirrored = z + upper * (3 - 2 * z)
    for place in (mirrored, 1 - mirrored, 2, 3):
        order.append(place + upper * (3 - 2 * place))

    def features(place, of_core):
        return pl.ds(pl.multiple_of((place * 2 + of_core) * width, width), width)

    for read in reads:
        read.start()
    weight_reads = [
        pltpu.make_async_copy(weight_hbm.at[features(place, core)], weight.at[place], local_sems.at[len(reads) + n])
        for n, place in enumerate(order)
    ]
    for read in weight_reads:
        read.start()

    plane = [((section + k // 2) % sections, (tensor // 2) * 2 + (core + k) % 2) for k in range(1, 8)]
    line = [(section, (tensor + k) % tensors) for k in range(1, 8)]
    barrier = pltpu.get_barrier_semaphore()
    greeted = plane + [(section, ((z + k) % 4) * 2 + c) for k in range(1, 4) for c in range(2)]
    for peer in greeted:
        pl.semaphore_signal(barrier, inc=1, device_id=peer, device_id_type=MESH)

    reads[0].wait()
    widened = rows_all[own].astype(jnp.float32)
    squares = jnp.sum(widened * widened, axis=1, keepdims=True)
    laid = jnp.transpose(jnp.broadcast_to(squares, (height, 128)))[0:8, :]
    parts[pl.ds(tensor, 1)] = laid[None]
    pl.semaphore_wait(barrier, len(greeted))

    unconditional = []
    conditional = []

    def push(source, target, receive, peer, when=None):
        if when is None:
            copy = pltpu.make_async_remote_copy(
                src_ref=source,
                dst_ref=target,
                send_sem=send_sems.at[len(unconditional)],
                recv_sem=receive,
                device_id=peer,
                device_id_type=MESH,
            )
            unconditional.append(copy)
            copy.start()
        else:
            copy = pltpu.make_async_remote_copy(
                src_ref=source,
                dst_ref=target,
                send_sem=line_sems.at[len(conditional)],
                recv_sem=receive,
                device_id=peer,
                device_id_type=MESH,
            )
            conditional.append((when, copy))
            pl.when(when)(copy.start)

    def arrived(target, receive):
        pltpu.make_async_remote_copy(
            src_ref=target,
            dst_ref=target,
            send_sem=send_sems.at[0],
            recv_sem=receive,
            device_id=(section, twin),
            device_id_type=MESH,
        ).wait_recv()

    def send_weight(step):
        place = order[step]
        source = weight_hbm.at[features(place, 1 - core)]
        push(source, twin_weight.at[place], weight_sems.at[place], (section, twin))

    for peer in line:
        push(parts.at[tensor], parts.at[tensor], parts_sems.at[tensor], peer)
    reads[4].wait()
    for k in range(1, 4):
        push(gains.at[z], gains.at[z], gain_sems.at[z], (section, ((z + k) % 4) * 2 + core))

    first = height * 3 // 4
    tail = pl.ds(first, height - first)

    def halves(step):
        size = (first if step else height) // 2
        return pl.ds(0, size), pl.ds(size, size)

    def along(piece, receive, place):
        push(piece, piece, receive, (section, tensor + 2), (place <= z) & (z < 3))
        push(piece, piece, receive, (section, tensor - 2), (place >= z) & (z > 0))

    def pass_whole(step):
        block = section * 4 + order[step]
        along(rows_all.at[block], recv_sems.at[block, 0], order[step])

    def send_round(step):
        block = section * 4 + order[step]
        for peer, parts_in_order in ((beside_x, (0, 1)), (beside_y, (1, 0))):
            for part in parts_in_order:
                piece = rows_all.at[block, halves(step)[part]]
                push(piece, piece, recv_sems.at[block, part], (peer, tensor))

    pass_whole(0)
    send_round(0)

    reads[3].wait()
    states = lax.broadcasted_iota(jnp.int32, (table.shape[0], height), 0)
    one_hot = jnp.transpose((states == state_ref[...]).astype(jnp.float32)).astype(jnp.bfloat16)
    reads[1].wait()
    reads[2].wait()
    state_rows = jnp.dot(one_hot, table[...], preferred_element_type=jnp.float32)
    merged[...] = (embed[...].astype(jnp.float32) + state_rows).astype(jnp.bfloat16)
    push(merged, next_hbm, next_sem, ((section + 1) % sections, tensor))

    send_weight(0)

    for step in range(1, 4):
        send_weight(step)

    for _, peer in line:
        arrived(parts.at[peer], parts_sems.at[peer])
    squares_total = jnp.sum(parts[...], axis=0)
    factors[pl.ds(section, 1)] = lax.rsqrt(squares_total / (width * tensors) + EPSILON)[None]
    for peer in others:
        push(factors.at[section], factors.at[section], factor_sems.at[section], (peer, tensor))

    def multiply(source, step):
        place = order[step]
        row = pl.ds(pl.multiple_of(source * height, height), height)
        if step == 0 and source is not section:
            arrived(factors.at[source], factor_sems.at[source])
        factor = jnp.transpose(jnp.broadcast_to(factors[source][0:1, :], (height, height)))[:, 0:1]
        widened = rows_all[source * 4 + place].astype(jnp.float32)
        block = (widened * factor * gains[place]).astype(jnp.bfloat16)
        for sums, by in ((twin_total, twin_weight), (total, weight)):
            product = jnp.dot(block, by[place], preferred_element_type=jnp.float32)
            if step:
                product += sums[row, :]
            sums[row, :] = product
            if step == 3 and sums is twin_total:
                push(twin_total.at[row], from_twin.at[row], total_sems.at[source], (section, twin))

    def weights_there(step):
        weight_reads[step].wait()
        arrived(twin_weight.at[order[step]], weight_sems.at[order[step]])

    middle, outer = mirrored == 1, mirrored == 0

    def whole_there(step, when=None):
        block = section * 4 + order[step]
        wait = functools.partial(arrived, rows_all.at[block], recv_sems.at[block, 0])
        if when is None:
            wait()
        else:
            pl.when(when)(wait)

    def from_line(step):
        if step:
            send_round(step)
            arrived(gains.at[order[step]], gain_sems.at[order[step]])
        weights_there(step)
        multiply(section, step)

    def tails(sources, step, when=None):
        for source in sources:
            block = source * 4 + order[step]
            piece = rows_all.at[block, tail]
            if step:
                wait = functools.partial(arrived, piece, recv_sems.at[block, 2])
                if when is None:
                    wait()
                else:
                    pl.when(when)(wait)
            if when is not outer:
                along(piece, recv_sems.at[block, 2], order[step])

    def from_beside(step):
        for source, onward, part in ((beside_x, beside_y, 0), (beside_y, beside_x, 1)):
            block = source * 4 + order[step]
            piece = rows_all.at[block, halves(step)[part]]
            arrived(piece, recv_sems.at[block, part])
            push(piece, piece, recv_sems.at[block, part], (onward, tensor))
        for source, part in ((beside_x, 1), (beside_y, 0)):
            block = source * 4 + order[step]
            piece = rows_all.at[block, halves(step)[part]]
            arrived(piece, recv_sems.at[block, part])
            if step == 0:
                tails((source,), 0)
        multiply(beside_x, step)
        multiply(beside_y, step)

    def from_across(step):
        block = across * 4 + order[step]
        for part in range(2):
            arrived(rows_all.at[block, halves(step)[part]], recv_sems.at[block, part])
        if step == 0:
            tails((across,), 0)
        multiply(across, step)

    from_line(0)
    whole_there(1)
    pass_whole(1)
    from_line(1)
    whole_there(2, middle)
    pass_whole(2)
    from_beside(0)
    whole_there(2, outer)
    from_line(2)
    from_across(0)
    whole_there(3, middle)
    pass_whole(3)
    tails(others, 1)
    tails(others, 2, middle)
    from_beside(1)
    whole_there(3, outer)
    from_line(3)
    tails(others, 3, middle)
    from_across(1)
    tails(others, 2, outer)
    from_beside(2)
    tails(others, 3, outer)
    from_across(2)
    from_beside(3)
    from_across(3)

    for read in reads[5:]:
        read.wait()
    for source in (section, *others):
        row = pl.ds(pl.multiple_of(source * height, height), height)
        arrived(from_twin.at[row], total_sems.at[source])
    logits = jnp.transpose(total[...] + from_twin[...])
    slots = lax.broadcasted_iota(jnp.int32, tiles_ref.shape, 0)
    live = slots < count_ref[...]
    own_tiles = columns // TILE
    hits = []
    for n in range(own_tiles):
        match = live & (tiles_ref[...] == device * own_tiles + n)
        hits.append(jnp.max(match.astype(jnp.int32), axis=0, keepdims=True) > 0)
    blocks = [logits[n * TILE:(n + 1) * TILE, :] for n in range(own_tiles)]
    largest = jnp.full(count_ref.shape, LOWEST, jnp.float32)
    for hit, block in zip(hits, blocks):
        largest = jnp.maximum(largest, jnp.where(hit, jnp.max(block, axis=0, keepdims=True), LOWEST))
    terms = jnp.zeros_like(largest)
    for hit, block in zip(hits, blocks):
        terms += jnp.where(hit, jnp.sum(jnp.exp(block - largest), axis=0, keepdims=True), 0.0)
    place = lax.broadcasted_iota(jnp.int32, logits.shape, 0)
    chosen = jnp.sum(jnp.where(place == token_ref[...] - device * columns, logits, 0.0), axis=0, keepdims=True)

    def packed(largest, terms, chosen):
        line = lax.broadcasted_iota(jnp.int32, (8, largest.shape[1]), 0)
        return jnp.where(line == 0, largest, jnp.where(line == 1, terms, jnp.where(line == 2, chosen, 0.0)))

    def combined(stats):
        values = [stats[n] for n in range(stats.shape[0])]
        largest = functools.reduce(jnp.maximum, [value[0:1, :] for value in values])
        terms = sum(value[1:2, :] * jnp.exp(value[0:1, :] - largest) for value in values)
        chosen = sum(value[2:3, :] for value in values)
        return largest, terms, chosen

    slot = section * 2 + core
    plane_stats[pl.ds(slot, 1)] = packed(largest, terms, chosen)[None]
    for peer in plane:
        push(plane_stats.at[slot], plane_stats.at[slot], plane_sems.at[slot], peer)
    for peer_section, peer_tensor in plane:
        peer_slot = peer_section * 2 + peer_tensor % 2
        arrived(plane_stats.at[peer_slot], plane_sems.at[peer_slot])
    line_stats[pl.ds(z, 1)] = packed(*combined(plane_stats))[None]
    for k in range(1, 4):
        push(line_stats.at[z], line_stats.at[z], line_stat_sems.at[z], (section, ((z + k) % 4) * 2 + core))
    for k in range(1, 4):
        peer_z = (z + k) % 4
        arrived(line_stats.at[peer_z], line_stat_sems.at[peer_z])
    largest, terms, chosen = combined(line_stats)
    stats_ref[...] = packed(largest + jnp.log(terms), chosen, chosen)

    arrived(next_hbm, next_sem)
    for copy in unconditional:
        copy.wait_send()
    for when, copy in conditional:
        pl.when(when)(copy.wait_send)


def block_shards(
    hidden,
    norm_gain,
    head_weight,
    tile_list,
    tile_count,
    chosen_token,
    chosen_embed,
    stack_state,
    state_table,
):
    height, width = hidden.shape
    row_count = tile_count.shape[0]
    columns = head_weight.shape[1]
    dma = pltpu.SemaphoreType.DMA
    stats, next_input = pl.pallas_call(
        head_kernel,
        out_shape=(
            jax.ShapeDtypeStruct((8, row_count), jnp.float32),
            jax.ShapeDtypeStruct(chosen_embed.shape, jnp.bfloat16),
        ),
        in_specs=[HBM] * 9,
        out_specs=(VMEM, ANY),
        scratch_shapes=[
            pltpu.VMEM((16, height, width), jnp.bfloat16),
            pltpu.VMEM((4, width, columns), jnp.bfloat16),
            pltpu.VMEM((4, width, columns), jnp.bfloat16),
            pltpu.VMEM((row_count, columns), jnp.float32),
            pltpu.VMEM((row_count, columns), jnp.float32),
            pltpu.VMEM((row_count, columns), jnp.float32),
            pltpu.VMEM(chosen_embed.shape, jnp.bfloat16),
            pltpu.VMEM(state_table.shape, jnp.bfloat16),
            pltpu.VMEM(chosen_embed.shape, jnp.bfloat16),
            pltpu.VMEM((4, 1, width), jnp.float32),
            pltpu.VMEM((4, 8, height), jnp.float32),
            pltpu.VMEM(tile_list.shape[::-1], jnp.int32),
            pltpu.VMEM((1, row_count), jnp.int32),
            pltpu.VMEM((1, row_count), jnp.int32),
            pltpu.VMEM((1, height), jnp.int32),
            pltpu.VMEM((8, 8, height), jnp.float32),
            pltpu.VMEM((8, 8, row_count), jnp.float32),
            pltpu.VMEM((4, 8, row_count), jnp.float32),
            dma((80,)),
            dma((32,)),
            dma((16, 3)),
            dma((4,)),
            dma((4,)),
            dma((4,)),
            dma((4,)),
            dma,
            dma((8,)),
            dma((8,)),
            dma((4,)),
            dma((12,)),
        ],
        compiler_params=pltpu.CompilerParams(
            collective_id=0, has_side_effects=True, vmem_limit_bytes=60 * 1024 * 1024
        ),
        name="masked_head",
    )(
        hidden,
        norm_gain[None, :],
        head_weight,
        tile_list.T,
        tile_count[None, :],
        chosen_token[None, :],
        chosen_embed,
        stack_state[None, :],
        state_table,
    )
    return (stats[1] - stats[0], stats[0], next_input)


def solution(mesh):
    placed = (
        P("section", "tensor"),
        P("tensor"),
        P(None, ("section", "tensor")),
        P(),
        P(),
        P(),
        P("section", "tensor"),
        P("section"),
        P(None, "tensor"),
    )
    small = mesh.shape["section"] == 4 and mesh.shape["tensor"] == 8
    return jax.shard_map(
        block_shards if small else shards,
        mesh=mesh,
        in_specs=placed,
        out_specs=(P(), P(), P("section", "tensor")),
        check_vma=False,
    )
```

```python
import functools

import jax
import jax.numpy as jnp
from jax import lax
from jax.experimental import pallas as pl
from jax.experimental.pallas import tpu as pltpu
from jax.sharding import PartitionSpec as P

D = 16384
TILE = 128
TILES_DEV = 2


EPSILON = 1e-05
NEG_FILL = -1e30


def shifted_2(value, axis, steps):
    count = lax.axis_size(axis)
    pairs = [(source, (source + steps) % count) for source in range(count)]
    return lax.ppermute(value, axis, pairs)


def scale_rows(widened, squares_total, width, gain):
    factor = lax.rsqrt(squares_total / width + EPSILON)
    return (widened * factor[:, None] * gain[None, :]).astype(jnp.bfloat16)


def shards(
    hidden,
    norm_gain,
    head_weight,
    tile_list,
    tile_count,
    chosen_token,
    chosen_embed,
    stack_state,
    state_table,
):
    states = jnp.arange(state_table.shape[0], dtype=jnp.int32)
    one_hot = (stack_state[:, None] == states[None, :]).astype(jnp.bfloat16)
    state_rows = jnp.dot(one_hot, state_table, preferred_element_type=jnp.float32)
    merged = (chosen_embed.astype(jnp.float32) + state_rows).astype(jnp.bfloat16)
    next_input = shifted_2(merged, "section", 1)
    widened = hidden.astype(jnp.float32)
    squares_total = lax.psum(jnp.sum(widened * widened, axis=1), "tensor")
    normed = scale_rows(widened, squares_total, D, norm_gain)
    all_rows = lax.all_gather(normed, "section", axis=0, tiled=True)
    logits = jnp.dot(
        lax.all_gather(all_rows, "tensor", axis=1, tiled=True),
        head_weight,
        preferred_element_type=jnp.float32,
    )
    row_count = logits.shape[0]
    vocab_here = logits.shape[1]
    device = lax.axis_index("section") * lax.axis_size("tensor") + lax.axis_index("tensor")
    own_tiles = device * TILES_DEV + jnp.arange(TILES_DEV, dtype=jnp.int32)
    live_slot = jnp.arange(tile_list.shape[1], dtype=jnp.int32)[None, :] < tile_count[:, None]
    matches = (tile_list[:, :, None] == own_tiles[None, None, :]) & live_slot[:, :, None]
    allowed = jnp.any(matches, axis=1)
    blocks = logits.reshape(row_count, TILES_DEV, TILE)
    allowed_mask = jnp.broadcast_to(allowed[:, :, None], blocks.shape)
    local_top = jnp.max(jnp.where(allowed_mask, blocks, NEG_FILL), axis=(1, 2))
    column = chosen_token - device * vocab_here
    columns = jnp.arange(vocab_here, dtype=jnp.int32)
    picked = jnp.sum(jnp.where(columns[None, :] == column[:, None], logits, 0.0), axis=1)
    row_top = lax.pmax(local_top, ("section", "tensor"))
    shifted = jnp.where(allowed_mask, blocks - row_top[:, None, None], NEG_FILL)
    terms = jnp.sum(jnp.exp(shifted), axis=(1, 2))
    totals, chosen_logit = lax.psum((terms, picked), ("section", "tensor"))
    normalizer = row_top + jnp.log(totals)
    log_prob = chosen_logit - normalizer
    return (log_prob, normalizer, next_input)


LOWEST = -3e38
MESH = pl.DeviceIdType.MESH
HBM = pl.BlockSpec(memory_space=pltpu.HBM)
ANY = pl.BlockSpec(memory_space=pl.ANY)
VMEM = pl.BlockSpec(memory_space=pltpu.VMEM)


def head_kernel(
    hidden_hbm,
    gain_hbm,
    weight_hbm,
    tiles_hbm,
    count_hbm,
    token_hbm,
    embed_hbm,
    state_hbm,
    table_hbm,
    stats_ref,
    next_hbm,
    rows_all,
    weight,
    twin_weight,
    total,
    twin_total,
    from_twin,
    embed,
    table,
    merged,
    gains,
    factors,
    tiles_ref,
    count_ref,
    token_ref,
    state_ref,
    parts,
    plane_stats,
    line_stats,
    send_sems,
    line_sems,
    recv_sems,
    weight_sems,
    total_sems,
    gain_sems,
    factor_sems,
    next_sem,
    parts_sems,
    plane_sems,
    line_stat_sems,
    local_sems,
):
    section = lax.axis_index("section")
    tensor = lax.axis_index("tensor")
    sections = 4
    tensors = 8
    x, y = section % 2, section // 2
    z, core = tensor // 2, tensor % 2
    beside_x = section + 1 - 2 * x
    beside_y = section + 2 - 4 * y
    across = 3 - section
    others = (beside_x, beside_y, across)
    twin = tensor + 1 - 2 * core
    height, width = embed.shape
    columns = weight.shape[2]
    device = section * tensors + tensor

    own = section * 4 + z

    reads = [
        pltpu.make_async_copy(source, target, local_sems.at[n])
        for n, (source, target) in enumerate(
            (
                (hidden_hbm, rows_all.at[own]),
                (table_hbm, table),
                (embed_hbm, embed),
                (state_hbm, state_ref),
                (gain_hbm, gains.at[z]),
                (tiles_hbm, tiles_ref),
                (count_hbm, count_ref),
                (token_hbm, token_ref),
            )
        )
    ]
    upper = z // 2
    order = []
    mirrored = z + upper * (3 - 2 * z)
    for place in (mirrored, 1 - mirrored, 2, 3):
        order.append(place + upper * (3 - 2 * place))

    def features(place, of_core):
        return pl.ds(pl.multiple_of((place * 2 + of_core) * width, width), width)

    for read in reads:
        read.start()
    weight_reads = [
        pltpu.make_async_copy(weight_hbm.at[features(place, core)], weight.at[place], local_sems.at[len(reads) + n])
        for n, place in enumerate(order)
    ]
    for read in weight_reads:
        read.start()

    plane = [((section + k // 2) % sections, (tensor // 2) * 2 + (core + k) % 2) for k in range(1, 8)]
    line = [(section, (tensor + k) % tensors) for k in range(1, 8)]
    barrier = pltpu.get_barrier_semaphore()
    greeted = plane + [(section, ((z + k) % 4) * 2 + c) for k in range(1, 4) for c in range(2)]
    for peer in greeted:
        pl.semaphore_signal(barrier, inc=1, device_id=peer, device_id_type=MESH)

    reads[0].wait()
    widened = rows_all[own].astype(jnp.float32)
    squares = jnp.sum(widened * widened, axis=1, keepdims=True)
    laid = jnp.transpose(jnp.broadcast_to(squares, (height, 128)))[0:8, :]
    parts[pl.ds(tensor, 1)] = laid[None]
    pl.semaphore_wait(barrier, len(greeted))

    unconditional = []
    conditional = []

    def push(source, target, receive, peer, when=None):
        if when is None:
            copy = pltpu.make_async_remote_copy(
                src_ref=source,
                dst_ref=target,
                send_sem=send_sems.at[len(unconditional)],
                recv_sem=receive,
                device_id=peer,
                device_id_type=MESH,
            )
            unconditional.append(copy)
            copy.start()
        else:
            copy = pltpu.make_async_remote_copy(
                src_ref=source,
                dst_ref=target,
                send_sem=line_sems.at[len(conditional)],
                recv_sem=receive,
                device_id=peer,
                device_id_type=MESH,
            )
            conditional.append((when, copy))
            pl.when(when)(copy.start)

    def arrived(target, receive):
        pltpu.make_async_remote_copy(
            src_ref=target,
            dst_ref=target,
            send_sem=send_sems.at[0],
            recv_sem=receive,
            device_id=(section, twin),
            device_id_type=MESH,
        ).wait_recv()

    def send_weight(step):
        place = order[step]
        source = weight_hbm.at[features(place, 1 - core)]
        push(source, twin_weight.at[place], weight_sems.at[place], (section, twin))

    for peer in line:
        push(parts.at[tensor], parts.at[tensor], parts_sems.at[tensor], peer)
    reads[4].wait()
    for k in range(1, 4):
        push(gains.at[z], gains.at[z], gain_sems.at[z], (section, ((z + k) % 4) * 2 + core))

    first = height * 3 // 4
    tail = pl.ds(first, height - first)

    def halves(step):
        size = (first if step else height) // 2
        return pl.ds(0, size), pl.ds(size, size)

    middle, outer = mirrored == 1, mirrored == 0

    def along(piece, receive, place, there=None):
        up, down = (place <= z) & (z < 3), (place >= z) & (z > 0)
        if there is not None:
            up, down = up & there, down & there
        push(piece, piece, receive, (section, tensor + 2), up)
        push(piece, piece, receive, (section, tensor - 2), down)

    def pass_whole(step):
        block = section * 4 + order[step]
        along(rows_all.at[block], recv_sems.at[block, 0], order[step])

    def send_round(step):
        block = section * 4 + order[step]
        for peer, parts_in_order in ((beside_x, (0, 1)), (beside_y, (1, 0))):
            for part in parts_in_order:
                piece = rows_all.at[block, halves(step)[part]]
                push(piece, piece, recv_sems.at[block, part], (peer, tensor))

    pass_whole(0)
    send_round(0)

    reads[3].wait()
    states = lax.broadcasted_iota(jnp.int32, (table.shape[0], height), 0)
    one_hot = jnp.transpose((states == state_ref[...]).astype(jnp.float32)).astype(jnp.bfloat16)
    reads[1].wait()
    reads[2].wait()
    state_rows = jnp.dot(one_hot, table[...], preferred_element_type=jnp.float32)
    merged[...] = (embed[...].astype(jnp.float32) + state_rows).astype(jnp.bfloat16)
    push(merged, next_hbm, next_sem, ((section + 1) % sections, tensor))

    send_weight(0)

    for step in range(1, 4):
        send_weight(step)

    for _, peer in line:
        arrived(parts.at[peer], parts_sems.at[peer])
    squares_total = jnp.sum(parts[...], axis=0)
    factors[pl.ds(section, 1)] = lax.rsqrt(squares_total / (width * tensors) + EPSILON)[None]
    for peer in others:
        push(factors.at[section], factors.at[section], factor_sems.at[section], (peer, tensor))

    def multiply(source, step):
        place = order[step]
        row = pl.ds(pl.multiple_of(source * height, height), height)
        if step == 0 and source is not section:
            arrived(factors.at[source], factor_sems.at[source])
        factor = jnp.transpose(jnp.broadcast_to(factors[source][0:1, :], (height, height)))[:, 0:1]
        widened = rows_all[source * 4 + place].astype(jnp.float32)
        block = (widened * factor * gains[place]).astype(jnp.bfloat16)
        for sums, by in ((twin_total, twin_weight), (total, weight)):
            product = jnp.dot(block, by[place], preferred_element_type=jnp.float32)
            if step:
                product += sums[row, :]
            sums[row, :] = product
            if step == 3 and sums is twin_total:
                push(twin_total.at[row], from_twin.at[row], total_sems.at[source], (section, twin))

    def weights_there(step):
        weight_reads[step].wait()
        arrived(twin_weight.at[order[step]], weight_sems.at[order[step]])

    def whole_there(step, when=None):
        block = section * 4 + order[step]
        wait = functools.partial(arrived, rows_all.at[block], recv_sems.at[block, 0])
        if when is None:
            wait()
        else:
            pl.when(when)(wait)

    def from_line(step):
        if step:
            send_round(step)
            arrived(gains.at[order[step]], gain_sems.at[order[step]])
        weights_there(step)
        multiply(section, step)

    def tails(sources, step, when=None):
        for source in sources:
            block = source * 4 + order[step]
            piece = rows_all.at[block, tail]
            if step:
                wait = functools.partial(arrived, piece, recv_sems.at[block, 2])
                if when is None:
                    wait()
                else:
                    pl.when(when)(wait)
            if when is not outer or step == 0:
                along(piece, recv_sems.at[block, 2], order[step], when)

    def from_beside(step):
        for source, onward, part in ((beside_x, beside_y, 0), (beside_y, beside_x, 1)):
            block = source * 4 + order[step]
            piece = rows_all.at[block, halves(step)[part]]
            arrived(piece, recv_sems.at[block, part])
            push(piece, piece, recv_sems.at[block, part], (onward, tensor))
        for source, part in ((beside_x, 1), (beside_y, 0)):
            block = source * 4 + order[step]
            piece = rows_all.at[block, halves(step)[part]]
            arrived(piece, recv_sems.at[block, part])
            if step == 0:
                tails((source,), 0, outer)
        multiply(beside_x, step)
        multiply(beside_y, step)

    def from_across(step):
        block = across * 4 + order[step]
        for part in range(2):
            arrived(rows_all.at[block, halves(step)[part]], recv_sems.at[block, part])
        if step == 0:
            tails((across,), 0, outer)
        multiply(across, step)

    from_line(0)
    whole_there(1)
    pass_whole(1)
    from_line(1)
    whole_there(2, middle)
    pass_whole(2)
    from_beside(0)
    whole_there(2, outer)
    from_line(2)
    whole_there(3, middle)
    pass_whole(3)
    from_across(0)
    tails(others, 0, middle)
    tails(others, 1)
    tails(others, 2, middle)
    from_beside(1)
    whole_there(3, outer)
    from_line(3)
    tails(others, 3, middle)
    from_across(1)
    tails(others, 2, outer)
    from_beside(2)
    tails(others, 3, outer)
    from_across(2)
    from_beside(3)
    from_across(3)

    for read in reads[5:]:
        read.wait()
    for source in (section, *others):
        row = pl.ds(pl.multiple_of(source * height, height), height)
        arrived(from_twin.at[row], total_sems.at[source])
    logits = jnp.transpose(total[...] + from_twin[...])
    slots = lax.broadcasted_iota(jnp.int32, tiles_ref.shape, 0)
    live = slots < count_ref[...]
    own_tiles = columns // TILE
    hits = []
    for n in range(own_tiles):
        match = live & (tiles_ref[...] == device * own_tiles + n)
        hits.append(jnp.max(match.astype(jnp.int32), axis=0, keepdims=True) > 0)
    blocks = [logits[n * TILE:(n + 1) * TILE, :] for n in range(own_tiles)]
    largest = jnp.full(count_ref.shape, LOWEST, jnp.float32)
    for hit, block in zip(hits, blocks):
        largest = jnp.maximum(largest, jnp.where(hit, jnp.max(block, axis=0, keepdims=True), LOWEST))
    terms = jnp.zeros_like(largest)
    for hit, block in zip(hits, blocks):
        terms += jnp.where(hit, jnp.sum(jnp.exp(block - largest), axis=0, keepdims=True), 0.0)
    place = lax.broadcasted_iota(jnp.int32, logits.shape, 0)
    chosen = jnp.sum(jnp.where(place == token_ref[...] - device * columns, logits, 0.0), axis=0, keepdims=True)

    def packed(largest, terms, chosen):
        line = lax.broadcasted_iota(jnp.int32, (8, largest.shape[1]), 0)
        return jnp.where(line == 0, largest, jnp.where(line == 1, terms, jnp.where(line == 2, chosen, 0.0)))

    def combined(stats):
        values = [stats[n] for n in range(stats.shape[0])]
        largest = functools.reduce(jnp.maximum, [value[0:1, :] for value in values])
        terms = sum(value[1:2, :] * jnp.exp(value[0:1, :] - largest) for value in values)
        chosen = sum(value[2:3, :] for value in values)
        return largest, terms, chosen

    slot = section * 2 + core
    plane_stats[pl.ds(slot, 1)] = packed(largest, terms, chosen)[None]
    for peer in plane:
        push(plane_stats.at[slot], plane_stats.at[slot], plane_sems.at[slot], peer)
    for peer_section, peer_tensor in plane:
        peer_slot = peer_section * 2 + peer_tensor % 2
        arrived(plane_stats.at[peer_slot], plane_sems.at[peer_slot])
    line_stats[pl.ds(z, 1)] = packed(*combined(plane_stats))[None]
    for k in range(1, 4):
        push(line_stats.at[z], line_stats.at[z], line_stat_sems.at[z], (section, ((z + k) % 4) * 2 + core))
    for k in range(1, 4):
        peer_z = (z + k) % 4
        arrived(line_stats.at[peer_z], line_stat_sems.at[peer_z])
    largest, terms, chosen = combined(line_stats)
    stats_ref[...] = packed(largest + jnp.log(terms), chosen, chosen)

    arrived(next_hbm, next_sem)
    for copy in unconditional:
        copy.wait_send()
    for when, copy in conditional:
        pl.when(when)(copy.wait_send)


def block_shards(
    hidden,
    norm_gain,
    head_weight,
    tile_list,
    tile_count,
    chosen_token,
    chosen_embed,
    stack_state,
    state_table,
):
    height, width = hidden.shape
    row_count = tile_count.shape[0]
    columns = head_weight.shape[1]
    dma = pltpu.SemaphoreType.DMA
    stats, next_input = pl.pallas_call(
        head_kernel,
        out_shape=(
            jax.ShapeDtypeStruct((8, row_count), jnp.float32),
            jax.ShapeDtypeStruct(chosen_embed.shape, jnp.bfloat16),
        ),
        in_specs=[HBM] * 9,
        out_specs=(VMEM, ANY),
        scratch_shapes=[
            pltpu.VMEM((16, height, width), jnp.bfloat16),
            pltpu.VMEM((4, width, columns), jnp.bfloat16),
            pltpu.VMEM((4, width, columns), jnp.bfloat16),
            pltpu.VMEM((row_count, columns), jnp.float32),
            pltpu.VMEM((row_count, columns), jnp.float32),
            pltpu.VMEM((row_count, columns), jnp.float32),
            pltpu.VMEM(chosen_embed.shape, jnp.bfloat16),
            pltpu.VMEM(state_table.shape, jnp.bfloat16),
            pltpu.VMEM(chosen_embed.shape, jnp.bfloat16),
            pltpu.VMEM((4, 1, width), jnp.float32),
            pltpu.VMEM((4, 8, height), jnp.float32),
            pltpu.VMEM(tile_list.shape[::-1], jnp.int32),
            pltpu.VMEM((1, row_count), jnp.int32),
            pltpu.VMEM((1, row_count), jnp.int32),
            pltpu.VMEM((1, height), jnp.int32),
            pltpu.VMEM((8, 8, height), jnp.float32),
            pltpu.VMEM((8, 8, row_count), jnp.float32),
            pltpu.VMEM((4, 8, row_count), jnp.float32),
            dma((80,)),
            dma((40,)),
            dma((16, 3)),
            dma((4,)),
            dma((4,)),
            dma((4,)),
            dma((4,)),
            dma,
            dma((8,)),
            dma((8,)),
            dma((4,)),
            dma((12,)),
        ],
        compiler_params=pltpu.CompilerParams(
            collective_id=0, has_side_effects=True, vmem_limit_bytes=60 * 1024 * 1024
        ),
        name="masked_head",
    )(
        hidden,
        norm_gain[None, :],
        head_weight,
        tile_list.T,
        tile_count[None, :],
        chosen_token[None, :],
        chosen_embed,
        stack_state[None, :],
        state_table,
    )
    return (stats[1] - stats[0], stats[0], next_input)


def solution(mesh):
    placed = (
        P("section", "tensor"),
        P("tensor"),
        P(None, ("section", "tensor")),
        P(),
        P(),
        P(),
        P("section", "tensor"),
        P("section"),
        P(None, "tensor"),
    )
    small = mesh.shape["section"] == 4 and mesh.shape["tensor"] == 8
    return jax.shard_map(
        block_shards if small else shards,
        mesh=mesh,
        in_specs=placed,
        out_specs=(P(), P(), P("section", "tensor")),
        check_vma=False,
    )
```
